128 devices in a mesh: dom: 32 (over x, y, core), tp: 4 (over z).
Axes of the slice: x: 4, y: 4, z: 4, core: 2. Of those that a mesh axis runs over, the one named last changes fastest.
Arguments:
- particle_suffix_cache: bfloat16 [2, 512, 512, 1024], P(None, 'dom', None, 'tp'), may hold values from -480 to 480
- hidden: bfloat16 [512, 2, 4096], P('dom'), may hold values from -6 to 6
- query_weight: bfloat16 [4096, 4096], P(None, 'tp'), may hold values from -0.09375 to 0.09375
- key_projection_weight: bfloat16 [4096, 1024], P(None, 'tp'), may hold values from -0.09375 to 0.09375
- value_projection_weight: bfloat16 [4096, 1024], P(None, 'tp'), may hold values from -0.09375 to 0.09375
- twist_weight: float32 [4096], P('tp'), may hold values from -6 to 6
- parent_twist: float32 [512], P('dom'), may hold values from -8 to 8
- log_ratio: float32 [512, 2], P('dom'), may hold values from -400 to 8
- ancestors: int32 [512], replicated, may hold values from 0 to 511, as said below
Outputs:
- resampled_cache: bfloat16 [2, 512, 512, 1024], P(None, 'dom', None, 'tp')
- fresh_token_entries: bfloat16 [2, 512, 2, 1024], P(None, 'dom', None, 'tp')
- attention: bfloat16 [512, 2, 4096], P('dom', None, 'tp')
- log_weights: float32 [512], P('dom')
The draws below stay inside these ranges and needn't reach their ends.
Inputs may be any that keep to these rules, and one draw needn't show every extreme that they name: An old particle's index that lies on the new particle's own index of dom or on one of the two beside it: ancestors[n] // 16 differs from n // 16 by at most one; offspring counts are uneven.
All inputs are finite; a program needn't handle non-finite values.
Results may differ from the reference program's by a relative error of at most 0.007.
The reference program's roundings to bfloat16 on the way count: a program that leaves them out, or rounds other values in their place, can miss the bound.
Values may be sent and summed in bfloat16 or wider, within the bound.
No kernel may reach another device: no remote copies, remote signals or barrier semaphores. Data moves between devices by JAX's collectives and lax.ppermute only.
A program may use at most 192 MiB of HBM per device.

```python
import math
import jax
import jax.numpy as jnp
from jax import lax

MODEL_WIDTH = 4096
QUERY_HEADS = 32
KEY_VALUE_HEADS = 8
HEAD_SIZE = 128
SUFFIX_LENGTH = 512
DECODE_STEPS = 2
PART_DEV = 16
PARTICLE_COUNT = 512


def draw_particle_suffix_cache(key, part):
    key = jax.random.fold_in(key, 11)
    random_noise_key = jax.random.fold_in(key, 0)
    cache_entries = jnp.clip(jax.random.normal(random_noise_key, (2, PARTICLE_COUNT, SUFFIX_LENGTH, KEY_VALUE_HEADS * HEAD_SIZE), jnp.float32), -6.0, 6.0)
    return cache_entries.astype(jnp.bfloat16)


def draw_log_ratio(key, part):
    key = jax.random.fold_in(key, 12)
    fraction = jnp.arange(PARTICLE_COUNT).astype(jnp.float32)[:, None] / PARTICLE_COUNT
    base = jax.random.uniform(key, (PARTICLE_COUNT, DECODE_STEPS), jnp.float32, -6.0, 0.0)
    ramp = 8.0 * fraction
    return base + ramp


def draw_ancestors(key, part):
    key = jax.random.fold_in(key, 13)
    pick_key, turn_key, left_key, right_key = jax.random.split(key, 4)
    window = 3 * PART_DEV
    slots = jnp.arange(PARTICLE_COUNT)
    device = slots // PART_DEV
    within = slots % PART_DEV
    uniform_pick = jax.random.randint(pick_key, (PARTICLE_COUNT,), 0, window)
    skewed = uniform_pick * uniform_pick // window
    turn = jax.random.randint(turn_key, (PARTICLE_COUNT // PART_DEV,), 0, window)
    offset = (skewed + turn[device]) % window - PART_DEV
    left = -1 - jax.random.randint(left_key, (PARTICLE_COUNT,), 0, PART_DEV)
    right = PART_DEV + jax.random.randint(right_key, (PARTICLE_COUNT,), 0, PART_DEV)
    offset = jnp.where(within == 0, left, jnp.where(within == PART_DEV - 1, right, offset))
    picked = jnp.clip(device * PART_DEV + offset, 0, PARTICLE_COUNT - 1)
    return picked.astype(jnp.int32)


def block_levels(key, shape, shards, least, high):
    def one(dim, blocks):
        heights = jax.random.uniform(jax.random.fold_in(jax.random.fold_in(key, 6), dim), (blocks,), jnp.float32, least / len(shards), high / len(shards))
        return jnp.repeat(jnp.exp(heights), shape[dim] // blocks).reshape((-1,) + (1,) * (len(shape) - dim - 1))

    gain = one(*shards[0])
    for cut in shards[1:]:
        gain = gain * one(*cut)
    return gain


def noise(key, shape, deviation, most, cuts=(), dtype=jnp.bfloat16):
    result = deviation * jax.random.normal(key, shape, jnp.float32)
    if cuts:
        result = result * block_levels(key, shape, cuts, -0.22, 0.18)
    return jnp.clip(result, -most, most).astype(dtype)


def setup_inputs(seed: int = 0) -> dict:
    key_list = jax.random.split(jax.random.key(seed), 10)
    particle_suffix_cache = draw_particle_suffix_cache(jax.random.fold_in(key_list[9], 71), 0)
    hidden = noise(key_list[1], (PARTICLE_COUNT, DECODE_STEPS, MODEL_WIDTH), 1.0, 6.0, ((0, 32),))
    query_weight = noise(key_list[2], (MODEL_WIDTH, QUERY_HEADS * HEAD_SIZE), MODEL_WIDTH ** -0.5, 0.09375, ((1, 4),))
    key_projection_weight = noise(key_list[3], (MODEL_WIDTH, KEY_VALUE_HEADS * HEAD_SIZE), MODEL_WIDTH ** -0.5, 0.09375, ((1, 4),))
    value_projection_weight = noise(key_list[4], (MODEL_WIDTH, KEY_VALUE_HEADS * HEAD_SIZE), MODEL_WIDTH ** -0.5, 0.09375, ((1, 4),))
    twist_weight = noise(key_list[5], (QUERY_HEADS * HEAD_SIZE,), 1.0, 6.0, ((0, 4),), jnp.float32)
    parent_twist = noise(key_list[6], (PARTICLE_COUNT,), 2.0, 8.0, ((0, 32),), jnp.float32)
    log_ratio = draw_log_ratio(jax.random.fold_in(key_list[9], 71), 0)
    ancestors = draw_ancestors(jax.random.fold_in(key_list[9], 71), 0)
    return dict(particle_suffix_cache=particle_suffix_cache, hidden=hidden, query_weight=query_weight, key_projection_weight=key_projection_weight, value_projection_weight=value_projection_weight, twist_weight=twist_weight, parent_twist=parent_twist, log_ratio=log_ratio, ancestors=ancestors)


ROPE_BASE = 500000.0

def apply_rotary(tensor, anchor_point):
    half_dim = tensor.shape[-1] // 2
    step_count = tensor.shape[-3]
    positions = (anchor_point + jnp.arange(step_count)).astype(jnp.float32)
    frequency = jnp.exp(jnp.arange(half_dim).astype(jnp.float32) * (-2.0 * math.log(ROPE_BASE) / tensor.shape[-1]))
    angles = (positions[:, None] * frequency[None, :])[:, None, :]
    cosine = jnp.cos(angles)
    sine = jnp.sin(angles)
    first_half = tensor[..., :half_dim]
    second_half = tensor[..., half_dim:]
    return jnp.concatenate([first_half * cosine - second_half * sine, first_half * sine + second_half * cosine], -1)

def project_tokens(rows, weight):
    flat = rows.reshape(-1, rows.shape[-1])
    return jnp.dot(flat, weight, preferred_element_type=jnp.float32).reshape(rows.shape[0], rows.shape[1], -1)

def finish(query_vectors, weighted, maxima, totals, fresh_keys, fresh_values):
    score_scale = 1.0 / math.sqrt(query_vectors.shape[-1])
    new_scores = jnp.einsum('ntkgd,nukd->ntkgu', query_vectors, fresh_keys, preferred_element_type=jnp.float32) * score_scale
    step_count = query_vectors.shape[1]
    causal = jnp.arange(step_count)[:, None] >= jnp.arange(step_count)[None, :]
    new_scores = jnp.where(causal[None, :, None, None, :], new_scores, -jnp.inf)
    peak_score = jnp.maximum(maxima, lax.optimization_barrier(jnp.max(new_scores, -1)))
    carried = jnp.exp(maxima - peak_score)
    fresh = jnp.exp(new_scores - peak_score[..., None])
    numerator = carried[..., None] * weighted + jnp.einsum('ntkgu,nukd->ntkgd', fresh, fresh_values.astype(jnp.float32), precision=lax.Precision.HIGHEST)
    denominator = carried * totals + lax.optimization_barrier(jnp.sum(fresh, -1))
    return numerator / denominator[..., None]

def reference(particle_suffix_cache, hidden, query_weight, key_projection_weight, value_projection_weight, twist_weight, parent_twist, log_ratio, ancestors):
    query_group_size = QUERY_HEADS // KEY_VALUE_HEADS
    anchor_point = particle_suffix_cache.shape[2]
    parents = ancestors.astype(jnp.int32)
    resampled_cache = jnp.take(particle_suffix_cache, parents, axis=1)
    query_vectors = apply_rotary(project_tokens(hidden, query_weight).reshape(PARTICLE_COUNT, DECODE_STEPS, QUERY_HEADS, HEAD_SIZE), anchor_point).astype(jnp.bfloat16)
    query_vectors = query_vectors.reshape(PARTICLE_COUNT, DECODE_STEPS, KEY_VALUE_HEADS, query_group_size, HEAD_SIZE)
    fresh_keys = apply_rotary(project_tokens(hidden, key_projection_weight).reshape(PARTICLE_COUNT, DECODE_STEPS, KEY_VALUE_HEADS, HEAD_SIZE), anchor_point).astype(jnp.bfloat16)
    fresh_values = project_tokens(hidden, value_projection_weight).reshape(PARTICLE_COUNT, DECODE_STEPS, KEY_VALUE_HEADS, HEAD_SIZE).astype(jnp.bfloat16)
    key_lookup_table = particle_suffix_cache[0].reshape(PARTICLE_COUNT, SUFFIX_LENGTH, KEY_VALUE_HEADS, HEAD_SIZE)
    value_lookup_table = particle_suffix_cache[1].reshape(PARTICLE_COUNT, SUFFIX_LENGTH, KEY_VALUE_HEADS, HEAD_SIZE)
    score_scale = 1.0 / math.sqrt(HEAD_SIZE)

    def one_slot(inputs):
        slot_queries, parent = inputs
        key_rows = lax.dynamic_index_in_dim(key_lookup_table, parent, 0, keepdims=False)
        value_rows = lax.dynamic_index_in_dim(value_lookup_table, parent, 0, keepdims=False)
        scores = jnp.einsum('tkgd,lkd->tkgl', slot_queries, key_rows, preferred_element_type=jnp.float32) * score_scale
        maxima = lax.optimization_barrier(jnp.max(scores, -1))
        expo = jnp.exp(scores - maxima[..., None])
        totals = lax.optimization_barrier(jnp.sum(expo, -1))
        weighted = jnp.einsum('tkgl,lkd->tkgd', expo.astype(jnp.bfloat16), value_rows, preferred_element_type=jnp.float32)
        return (weighted, maxima, totals)
    weighted, maxima, totals = lax.map(one_slot, (query_vectors, parents))
    outputs = finish(query_vectors, weighted, maxima, totals, fresh_keys, fresh_values)
    attention = outputs.reshape(PARTICLE_COUNT, DECODE_STEPS, QUERY_HEADS * HEAD_SIZE).astype(jnp.bfloat16)
    twist_value = lax.optimization_barrier(jnp.sum(outputs[:, DECODE_STEPS - 1].reshape(PARTICLE_COUNT, QUERY_HEADS * HEAD_SIZE) * twist_weight[None, :], 1))
    log_weight = lax.optimization_barrier(jnp.sum(log_ratio, 1)) + twist_value - jnp.take(parent_twist, parents)
    peak = jnp.max(log_weight)
    log_weights = log_weight - (peak + jnp.log(jnp.sum(jnp.exp(log_weight - peak))))
    fresh_token_entries = jnp.stack([fresh_keys.reshape(PARTICLE_COUNT, DECODE_STEPS, KEY_VALUE_HEADS * HEAD_SIZE), fresh_values.reshape(PARTICLE_COUNT, DECODE_STEPS, KEY_VALUE_HEADS * HEAD_SIZE)])
    return (resampled_cache, fresh_token_entries, attention, log_weights)
```

```python
import functools
import math

import jax
import jax.numpy as jnp
import numpy as np
from jax import lax
from jax.experimental import pallas as pl
from jax.experimental.pallas import tpu as pltpu
from jax.sharding import PartitionSpec as P

HEAD_SIZE = 128
DECODE_STEPS = 2
ROPE_BASE = 500000.0
PIECES = (8,)
ALWAYS = sum(PIECES)
AT_ONCE = 4

SMEM = pl.BlockSpec(memory_space=pltpu.SMEM)
VMEM = pl.BlockSpec(memory_space=pltpu.VMEM)
ANY = pl.BlockSpec(memory_space=pl.ANY)
LIGHT = pl.CostEstimate(flops=0, bytes_accessed=0, transcendentals=0)


def chip_mate(d):
    return d + 1 - 2 * (d % 2)


def next_chip(d):
    return d - 1 + 2 * (d % 2)


def rope_tables(rows, anchor_point):
    half = HEAD_SIZE // 2
    frequency = np.exp(
        np.arange(half, dtype=np.float32) * np.float32(-2.0 * math.log(ROPE_BASE) / HEAD_SIZE)
    ).astype(np.float32)
    positions = (anchor_point + np.arange(rows) % DECODE_STEPS).astype(np.float32)
    angles = (positions[:, None] * frequency[None, :]).astype(np.float32)
    cosine = np.cos(angles).astype(np.float32)
    sine = np.sin(angles).astype(np.float32)
    return np.concatenate([cosine, cosine], 1), np.concatenate([-sine, sine], 1)


def bit_count(mask):
    mask = mask - ((mask >> 1) & 0x55555555)
    mask = (mask & 0x33333333) + ((mask >> 2) & 0x33333333)
    mask = (mask + (mask >> 4)) & 0x0F0F0F0F
    return (mask * 0x01010101) >> 24


def plan_kernel(peers, per_device, ancestors, grid, count, picks, ranks):
    d = lax.axis_index("dom")
    shape = grid.shape
    flat = lax.broadcasted_iota(jnp.int32, shape, 0) * shape[1] + lax.broadcasted_iota(
        jnp.int32, shape, 1
    )
    home = flat // per_device
    offset = grid[...] - next_chip(home) * per_device
    inside = (offset >= 0) & (offset < per_device)
    bits = jnp.where(inside, jnp.int32(1) << (offset & (per_device - 1)), 0)
    shift = 1
    while shift < per_device:
        bits = bits | pltpu.roll(bits, shape[1] - shift, 1)
        shift *= 2
    most = jnp.where(flat % per_device == 0, bit_count(bits), 0)
    count[0] = jnp.max(most.astype(jnp.float32)).astype(jnp.int32)

    def needed(home, owner):
        mask = jnp.int32(0)
        for k in range(per_device):
            offset = ancestors[home * per_device + k] - owner * per_device
            inside = (offset >= 0) & (offset < per_device)
            mask = mask | jnp.where(inside, jnp.int32(1) << (offset & (per_device - 1)), 0)
        return mask

    there = next_chip(d)
    mask = needed(jnp.clip(there, 0, peers - 1), d)
    position = jnp.int32(0)
    for j in range(per_device):
        picks[j] = 0
    for j in range(per_device):
        picks[position] = j
        position = position + ((mask >> j) & 1)
    mask = needed(d, there)
    for k in range(per_device):
        offset = ancestors[d * per_device + k] - there * per_device
        inside = (offset >= 0) & (offset < per_device)
        below = (jnp.int32(1) << (offset & (per_device - 1))) - 1
        ranks[k] = jnp.where(inside, bit_count(mask & below), -1)


def plan(ancestors, peers, per_device):
    return pl.pallas_call(
        functools.partial(plan_kernel, peers, per_device),
        out_shape=(
            jax.ShapeDtypeStruct((1,), jnp.int32),
            jax.ShapeDtypeStruct((per_device,), jnp.int32),
            jax.ShapeDtypeStruct((per_device,), jnp.int32),
        ),
        in_specs=[SMEM, VMEM],
        out_specs=(SMEM, SMEM, SMEM),
        cost_estimate=LIGHT,
        name="plan",
    )(ancestors, ancestors.reshape(-1, 128))


def gather_kernel(skip, size, picks, cache, sent, held, loads, stores):
    def load(i, c):
        return pltpu.make_async_copy(cache.at[c, picks[skip + i]], held.at[c, i], loads.at[c, i])

    def store(i, c):
        return pltpu.make_async_copy(held.at[c, i], sent.at[c, i], stores.at[c, i])

    def each(act):
        def body(i, carry):
            for c in range(2):
                act(i, c)
            return carry

        lax.fori_loop(0, size, body, 0)

    each(lambda i, c: load(i, c).start())

    def forward(i, c):
        load(i, c).wait()
        store(i, c).start()

    each(forward)
    each(lambda i, c: store(i, c).wait())


def gather(picks, cache, skip, size):
    shape = (2, size, *cache.shape[2:])
    return pl.pallas_call(
        functools.partial(gather_kernel, skip, size),
        out_shape=jax.ShapeDtypeStruct(shape, cache.dtype),
        in_specs=[SMEM, ANY],
        out_specs=ANY,
        scratch_shapes=[
            pltpu.VMEM(shape, cache.dtype),
            pltpu.SemaphoreType.DMA((2, size)),
            pltpu.SemaphoreType.DMA((2, size)),
        ],
        compiler_params=pltpu.CompilerParams(vmem_limit_bytes=20 * 2**20),
        cost_estimate=LIGHT,
        name="gather",
    )(picks, cache)


def place_kernel(per_device, find, numbers, *refs):
    *sources, out, held, loads, stores = refs
    d = lax.axis_index("dom")

    def each(act):
        def body(k, carry):
            for source, (there, at) in zip(sources, find(numbers, d, k)):

                @pl.when(there)
                def _():
                    for c in range(2):
                        act(source, at, k, c)

            return carry

        lax.fori_loop(0, per_device, body, 0)

    def load(source, at, k, c):
        return pltpu.make_async_copy(source.at[c, at], held.at[c, k], loads.at[c, k])

    def store(k, c):
        return pltpu.make_async_copy(held.at[c, k], out.at[c, k], stores.at[c, k])

    def forward(source, at, k, c):
        load(source, at, k, c).wait()
        store(k, c).start()

    each(lambda source, at, k, c: load(source, at, k, c).start())
    each(forward)
    each(lambda source, at, k, c: store(k, c).wait())


def place(find, numbers, sources, placed, name):
    per_device = placed.shape[1]
    operands = [numbers, *sources, placed]

    def kernel(*refs):
        refs = list(refs)
        del refs[1 + len(sources)]
        place_kernel(per_device, find, *refs)

    return pl.pallas_call(
        kernel,
        out_shape=pltpu.HBM(placed.shape, placed.dtype),
        in_specs=[SMEM] + [ANY] * (len(operands) - 1),
        out_specs=ANY,
        scratch_shapes=[
            pltpu.VMEM(placed.shape, placed.dtype),
            pltpu.SemaphoreType.DMA((2, per_device)),
            pltpu.SemaphoreType.DMA((2, per_device)),
        ],
        input_output_aliases={len(operands) - 1: 0},
        compiler_params=pltpu.CompilerParams(vmem_limit_bytes=20 * 2**20),
        cost_estimate=LIGHT,
        name=name,
    )(*operands)


def place_mate(ancestors, mate, placed):
    per_device = placed.shape[1]

    def find(ancestors, d, k):
        offset = ancestors[d * per_device + k] - chip_mate(d) * per_device
        yield (offset >= 0) & (offset < per_device), offset

    return place(find, ancestors, [mate], placed, "place_mate")


def place_far(ranks, came, placed, skip):
    size = came.shape[1]

    def find(ranks, d, k):
        rank = ranks[k] - skip
        yield (rank >= 0) & (rank < size), rank

    return place(find, ranks, [came], placed, "place_far")


def project_kernel(heads, groups, own, mate, far, wq, wk, wv, cosine, sine, *refs):
    *outs, keys, values, total, turned = refs
    step = pl.program_id(0)
    width_q, width_k = heads * HEAD_SIZE, groups * HEAD_SIZE
    rows = jnp.concatenate([own[...], mate[...], far[...]], 0)
    parts = (
        (wq, 0, width_q),
        (wk, width_q, width_k),
        (wv, width_q + width_k, width_k),
    )

    @pl.when(step == 0)
    def _():
        total[...] = jnp.zeros_like(total)

    for weight, at, width in parts:
        total[:, at : at + width] += jnp.dot(
            rows, weight[...], preferred_element_type=jnp.float32
        )

    @pl.when(step == pl.num_programs(0) - 1)
    def _():
        count = own.shape[0]
        queries = heads * count

        def turn(x):
            return x * cosine[...] + pltpu.roll(x, HEAD_SIZE // 2, 1) * sine[...]

        for h, packed in enumerate(outs):
            mine = slice(h * count, (h + 1) * count)
            for i in range(heads):
                turned[:, i, :] = turn(total[mine, i * HEAD_SIZE : (i + 1) * HEAD_SIZE])
            packed[:queries, :] = turned[...].reshape(queries, HEAD_SIZE).astype(packed.dtype)
            for g in range(groups):
                lanes = slice(g * HEAD_SIZE, (g + 1) * HEAD_SIZE)
                at = width_q + g * HEAD_SIZE
                key = turn(total[mine, at : at + HEAD_SIZE]).astype(packed.dtype)
                at = at + width_k
                value = total[mine, at : at + HEAD_SIZE].astype(packed.dtype)
                at = queries + g * count
                packed[at : at + count, :] = key
                at = queries + (groups + g) * count
                packed[at : at + count, :] = value
                if h == 0:
                    keys[:, lanes] = key
                    values[:, lanes] = value


def project(own, mate, far, wq, wk, wv, anchor_point):
    count, depth = own.shape
    heads, groups = wq.shape[1] // HEAD_SIZE, wk.shape[1] // HEAD_SIZE
    block = 1024
    cosine, sine = rope_tables(count, anchor_point)
    columns = wq.shape[1] + wk.shape[1] + wv.shape[1]
    whole = lambda *shape: pl.BlockSpec(shape, lambda i: (0, 0))
    rows = pl.BlockSpec((count, block), lambda i: (0, i))
    packed = ((heads + 2 * groups) * count, HEAD_SIZE)
    fresh = (count, groups * HEAD_SIZE)
    return pl.pallas_call(
        functools.partial(project_kernel, heads, groups),
        grid=(depth // block,),
        out_shape=[jax.ShapeDtypeStruct(shape, jnp.bfloat16) for shape in (packed,) * 3 + (fresh,) * 2],
        in_specs=[
            rows,
            rows,
            rows,
            pl.BlockSpec((block, wq.shape[1]), lambda i: (i, 0)),
            pl.BlockSpec((block, wk.shape[1]), lambda i: (i, 0)),
            pl.BlockSpec((block, wv.shape[1]), lambda i: (i, 0)),
            whole(count, HEAD_SIZE),
            whole(count, HEAD_SIZE),
        ],
        out_specs=[whole(*shape) for shape in (packed,) * 3 + (fresh,) * 2],
        scratch_shapes=[
            pltpu.VMEM((3 * count, columns), jnp.float32),
            pltpu.VMEM((count, heads, HEAD_SIZE), jnp.float32),
        ],
        compiler_params=pltpu.CompilerParams(vmem_limit_bytes=56 * 2**20),
        cost_estimate=LIGHT,
        name="project",
    )(own, mate, far, wq, wk, wv, cosine, sine)


def attend_kernel(
    peers, per_device, heads, groups,
    ancestors, parent_twist, log_ratio, twist_weight, own, mate, far, cache,
    out_own, out_mate, out_far, part, placed,
    held, tokens, fresh, results, lists, slots, owners, sems, stores,
):
    d = lax.axis_index("dom")
    first_lane = (lax.axis_index("tp") == 0).astype(jnp.float32)
    tile = DECODE_STEPS * heads
    queries = per_device * tile
    small = per_device * DECODE_STEPS
    homes = (d, chip_mate(d), next_chip(d))

    def load(j, c):
        return pltpu.make_async_copy(cache.at[c, j], held.at[c, j], sems.at[c, j])

    def begin(j, carry):
        for c in range(2):
            load(j, c).start()
        lists[j] = -1
        return carry

    lax.fori_loop(0, per_device, begin, 0)
    for h, home in enumerate(homes):
        there = (home >= 0) & (home < peers)
        start = jnp.clip(home, 0, peers - 1) * per_device

        def enlist(k, carry):
            offset = ancestors[start + k] - d * per_device

            @pl.when(there & (offset >= 0) & (offset < per_device))
            def _():
                slot = h * per_device + k
                lists[per_device + slot] = lists[offset]
                lists[offset] = slot

            return carry

        lax.fori_loop(0, per_device, enlist, 0)

    def flatten(j, count):
        def step(state):
            slot, count = state
            slots[count] = slot
            owners[count] = j
            return lists[per_device + slot], count + 1

        return lax.while_loop(lambda state: state[0] >= 0, step, (lists[j], count))[1]

    count = lax.fori_loop(0, per_device, flatten, jnp.int32(0))
    for extra in range(AT_ONCE - 1):

        @pl.when(count > 0)
        def _():
            slots[count + extra] = slots[count - 1]
            owners[count + extra] = owners[count - 1]

    part[...] = jnp.zeros_like(part)
    part[3 * per_device :, :DECODE_STEPS] = log_ratio[...] * first_lane
    results[...] = jnp.zeros_like(results)
    for h, source in enumerate((own, mate, far)):
        tokens[h * queries : (h + 1) * queries, :] = source[:queries, :]
        size = source.shape[0] - queries
        fresh[h * size : (h + 1) * size, :] = source[queries:, :].astype(jnp.float32)
    block = 2 * groups * small
    row = lax.broadcasted_iota(jnp.int32, (tile, 1), 0)
    lower = (row % heads) < heads // groups
    later = row >= heads
    lane = lax.broadcasted_iota(jnp.int32, (1, HEAD_SIZE), 1)
    scale = 1.0 / math.sqrt(HEAD_SIZE)
    twist = jnp.concatenate([jnp.zeros_like(twist_weight), twist_weight[...]], 0)

    def by_group(at):
        pair = [fresh[pl.ds(at + g * small, 1), :] for g in range(groups)]
        return jnp.where(lower, pair[0], pair[1])

    def scores_of(j, slot):
        query = tokens[pl.ds(pl.multiple_of(slot * tile, tile), tile), :]
        none = jnp.zeros_like(query)
        wide = jnp.concatenate([jnp.where(lower, query, none), jnp.where(lower, none, query)], 1)
        scores = (
            lax.dot_general(
                wide, held[0, j], (((1,), (1,)), ((), ())), preferred_element_type=jnp.float32
            )
            * scale
        )
        return query.astype(jnp.float32), scores

    def weights_of(scores):
        maxima = jnp.max(scores, 1, keepdims=True)
        expo = jnp.exp(scores - maxima)
        return maxima, expo

    def finish(j, slot, query, maxima, totals, both):
        weighted = jnp.where(lower, both[:, :HEAD_SIZE], both[:, HEAD_SIZE:])
        at = (slot // per_device) * block + (slot % per_device) * DECODE_STEPS
        new = [
            jnp.sum(query * by_group(at + u), 1, keepdims=True) * scale
            for u in range(DECODE_STEPS)
        ]
        new[1] = jnp.where(later, new[1], -jnp.inf)
        peak = jnp.maximum(maxima, jnp.maximum(new[0], new[1]))
        carried = jnp.exp(maxima - peak)
        numerator = carried * weighted
        denominator = carried * totals
        for u in range(DECODE_STEPS):
            share = jnp.exp(new[u] - peak)
            numerator = numerator + share * by_group(at + groups * small + u)
            denominator = denominator + share
        outputs = numerator / denominator
        results[pl.ds(pl.multiple_of(slot * tile, tile), tile), :] = outputs.astype(jnp.bfloat16)
        twisted = jnp.sum(outputs * twist, 0, keepdims=True)
        less = jnp.where(lane == 0, parent_twist[j] * first_lane, 0.0)
        part[pl.ds(slot, 1), :] = twisted - less

    def store(k, c):
        offset = ancestors[d * per_device + k] - d * per_device
        return pltpu.make_async_copy(held.at[c, offset], placed.at[c, k], stores.at[c, k])

    def each_own(act):
        def body(k, carry):
            offset = ancestors[d * per_device + k] - d * per_device

            @pl.when((offset >= 0) & (offset < per_device))
            def _():
                for c in range(2):
                    act(store(k, c))

            return carry

        lax.fori_loop(0, per_device, body, 0)

    def arrive(j, carry):
        for c in range(2):
            load(j, c).wait()
        return carry

    def serve(step, loaded):
        at = step * AT_ONCE
        last = owners[at + AT_ONCE - 1] + 1
        lax.fori_loop(loaded, last, arrive, 0)
        jobs = [(owners[at + i], slots[at + i]) for i in range(AT_ONCE)]
        scored = [scores_of(*job) for job in jobs]
        weights = [weights_of(scores) for _, scores in scored]
        totals = [jnp.sum(expo, 1, keepdims=True) for _, expo in weights]
        both = [
            jnp.dot(expo.astype(jnp.bfloat16), held[1, job[0]], preferred_element_type=jnp.float32)
            for job, (_, expo) in zip(jobs, weights)
        ]
        for i, job in enumerate(jobs):
            finish(*job, scored[i][0], weights[i][0], totals[i], both[i])
        return last

    loaded = lax.fori_loop(0, (count + AT_ONCE - 1) // AT_ONCE, serve, jnp.int32(0))
    lax.fori_loop(loaded, per_device, arrive, 0)
    each_own(lambda copy: copy.start())
    for h, out in enumerate((out_own, out_mate, out_far)):
        out[...] = results[h * queries : (h + 1) * queries, :]
    each_own(lambda copy: copy.wait())


def attend(ancestors, parent_twist, log_ratio, twist_weight, own, mate, far, cache, peers, heads, groups):
    per_device = cache.shape[1]
    tile = DECODE_STEPS * heads
    queries = per_device * tile
    block = own.shape[0] - queries
    result = jax.ShapeDtypeStruct((queries, HEAD_SIZE), jnp.bfloat16)
    return pl.pallas_call(
        functools.partial(attend_kernel, peers, per_device, heads, groups),
        out_shape=(
            result,
            result,
            result,
            jax.ShapeDtypeStruct((4 * per_device, HEAD_SIZE), jnp.float32),
            pltpu.HBM(cache.shape, cache.dtype),
        ),
        in_specs=[SMEM, SMEM, VMEM, VMEM, VMEM, VMEM, VMEM, ANY],
        out_specs=(VMEM, VMEM, VMEM, VMEM, ANY),
        scratch_shapes=[
            pltpu.VMEM(cache.shape, cache.dtype),
            pltpu.VMEM((3 * queries, HEAD_SIZE), jnp.bfloat16),
            pltpu.VMEM((3 * block, HEAD_SIZE), jnp.float32),
            pltpu.VMEM((3 * queries, HEAD_SIZE), jnp.bfloat16),
            pltpu.SMEM((4 * per_device,), jnp.int32),
            pltpu.SMEM((3 * per_device + AT_ONCE,), jnp.int32),
            pltpu.SMEM((3 * per_device + AT_ONCE,), jnp.int32),
            pltpu.SemaphoreType.DMA((2, per_device)),
            pltpu.SemaphoreType.DMA((2, per_device)),
        ],
        compiler_params=pltpu.CompilerParams(vmem_limit_bytes=24 * 2**20),
        cost_estimate=LIGHT,
        name="attend",
    )(ancestors, parent_twist, log_ratio, twist_weight, own, mate, far, cache)


def normalise_kernel(terms, *refs):
    *parts, out = refs
    del terms
    total = parts[0][...]
    for part in parts[1:]:
        total = total + part[...]
    peak = jnp.max(total, keepdims=True)
    mass = jnp.sum(jnp.exp(total - peak), keepdims=True)
    row = lax.broadcasted_iota(jnp.int32, total.shape, 0)
    mine = jnp.sum(jnp.where(row == lax.axis_index("dom"), total, 0.0), 0, keepdims=True)
    out[...] = mine - (peak + jnp.log(mass))


def normalise(parts):
    return pl.pallas_call(
        functools.partial(normalise_kernel, len(parts)),
        out_shape=jax.ShapeDtypeStruct((1, parts[0].shape[1]), jnp.float32),
        in_specs=[VMEM] * len(parts),
        out_specs=VMEM,
        cost_estimate=LIGHT,
        name="normalise",
    )(*parts)


def total_of(x, peers):
    chips = peers // 2
    side = math.isqrt(chips)
    on_chip = [(i, i ^ 1) for i in range(peers)]
    x = x + lax.ppermute(x, "dom", on_chip)
    ring = lax.axis_size("tp")
    x = x + sum(
        lax.ppermute(x, "tp", [(i, (i + hop) % ring) for i in range(ring)]) for hop in range(1, ring)
    )

    def along(i, axis):
        place = [i // (2 * side), i // 2 % side]
        place[axis] = (place[axis] + 1 - 2 * (i % 2)) % side
        return (place[0] * side + place[1]) * 2 + i % 2

    for axis in range(2):
        pairs = [(i, along(i, axis)) for i in range(peers)]
        first = lax.ppermute(x, "dom", pairs)
        parts = [x, first, lax.ppermute(first, "dom", pairs), lax.ppermute(first, "dom", on_chip)]
        x = sum(parts)
    return parts


def shards(
    cache,
    hidden,
    query_weight,
    key_projection_weight,
    value_projection_weight,
    twist_weight,
    parent_twist,
    log_ratio,
    ancestors,
):
    per_device = hidden.shape[0]
    heads = query_weight.shape[1] // HEAD_SIZE
    groups = key_projection_weight.shape[1] // HEAD_SIZE
    anchor_point = cache.shape[2]
    peers = lax.axis_size("dom")
    d = lax.axis_index("dom")
    on_chip = [(i, i ^ 1) for i in range(peers)]
    off_chip = [(i, i - 1 + 2 * (i % 2)) for i in range(1, peers - 1)]
    beside = [(i, i + 2 - 4 * (i % 2)) for i in range(peers) if 0 <= i + 2 - 4 * (i % 2) < peers]
    rows = hidden.reshape(per_device * DECODE_STEPS, -1)
    far_rows = lax.ppermute(rows, "dom", off_chip)
    mate_rows = lax.ppermute(rows, "dom", on_chip)
    count, picks, ranks = plan(ancestors, peers, per_device)
    came, skip = [], 0
    for size in PIECES:
        sent = gather(picks, cache, skip, size)
        if not came:
            sent, far_rows = lax.optimization_barrier((sent, far_rows))
        sent, picks = lax.optimization_barrier((sent, picks))
        came.append(lax.ppermute(sent, "dom", off_chip))
        skip += size
    mate_cache = lax.ppermute(cache, "dom", on_chip)
    own, mate, far, keys, values = project(
        rows, mate_rows, far_rows, query_weight, key_projection_weight, value_projection_weight,
        anchor_point,
    )
    own_part, mate_part, far_part, part, out = attend(
        ancestors, parent_twist, log_ratio, twist_weight.reshape(heads, HEAD_SIZE),
        own, mate, far, cache, peers, heads, groups,
    )
    part = jnp.sum(part, 1).reshape(4, per_device)
    index = jnp.arange(peers)[:, None]
    spread = jnp.where(
        index == d,
        part[0] + part[3],
        jnp.where(index == chip_mate(d), part[1], jnp.where(index == next_chip(d), part[2], 0.0)),
    )
    log_weights = normalise(total_of(spread, peers)).reshape(per_device)
    mate_part = lax.ppermute(mate_part, "dom", on_chip)
    far_part = lax.ppermute(far_part, "dom", on_chip)
    far_part = lax.ppermute(far_part, "dom", beside)
    owner = lax.dynamic_slice_in_dim(ancestors, d * per_device, per_device) // per_device
    owner = jnp.repeat(owner, DECODE_STEPS * heads)[:, None]
    attention = jnp.where(
        owner == d, own_part, jnp.where(owner == chip_mate(d), mate_part, far_part)
    ).reshape(per_device, DECODE_STEPS, heads * HEAD_SIZE)
    out = place_mate(ancestors, mate_cache, out)
    skip = 0
    for piece, size in zip(came, PIECES):
        out = place_far(ranks, piece, out, skip)
        skip += size
    fresh = jnp.stack([keys, values]).reshape(2, per_device, DECODE_STEPS, groups * HEAD_SIZE)

    def more(size):
        def branch(cache, picks, ranks, out):
            came = lax.ppermute(gather(picks, cache, ALWAYS, size), "dom", off_chip)
            return place_far(ranks, came, out, ALWAYS)

        return branch

    resampled_cache = lax.switch(
        jnp.maximum(count[0] - ALWAYS, 0),
        [lambda cache, picks, ranks, out: out] + [more(i + 1) for i in range(per_device - ALWAYS)],
        cache, picks, ranks, out,
    )
    return (resampled_cache, fresh, attention, log_weights)


def solution(mesh):
    return jax.shard_map(
        shards,
        mesh=mesh,
        in_specs=(
            P(None, "dom", None, "tp"),
            P("dom", None, None),
            P(None, "tp"),
            P(None, "tp"),
            P(None, "tp"),
            P("tp"),
            P("dom"),
            P("dom", None),
            P(),
        ),
        out_specs=(
            P(None, "dom", None, "tp"),
            P(None, "dom", None, "tp"),
            P("dom", None, "tp"),
            P("dom"),
        ),
        check_vma=False,
    )
```

```python
import functools
import math

import jax
import jax.numpy as jnp
import numpy as np
from jax import lax
from jax.experimental import pallas as pl
from jax.experimental.pallas import tpu as pltpu
from jax.sharding import PartitionSpec as P

HEAD_SIZE = 128
DECODE_STEPS = 2
ROPE_BASE = 500000.0
PIECES = (6, 2)
ALWAYS = sum(PIECES)
AT_ONCE = 4

SMEM = pl.BlockSpec(memory_space=pltpu.SMEM)
VMEM = pl.BlockSpec(memory_space=pltpu.VMEM)
ANY = pl.BlockSpec(memory_space=pl.ANY)
HBM = pl.BlockSpec(memory_space=pltpu.HBM)
SMALL = pltpu.CompilerParams(vmem_limit_bytes=2 * 2**20)
LIGHT = pl.CostEstimate(flops=0, bytes_accessed=0, transcendentals=0)


def chip_mate(d):
    return d + 1 - 2 * (d % 2)


def next_chip(d):
    return d - 1 + 2 * (d % 2)


def rope_tables(rows, anchor_point):
    half = HEAD_SIZE // 2
    frequency = np.exp(
        np.arange(half, dtype=np.float32) * np.float32(-2.0 * math.log(ROPE_BASE) / HEAD_SIZE)
    ).astype(np.float32)
    positions = (anchor_point + np.arange(rows) % DECODE_STEPS).astype(np.float32)
    angles = (positions[:, None] * frequency[None, :]).astype(np.float32)
    cosine = np.cos(angles).astype(np.float32)
    sine = np.sin(angles).astype(np.float32)
    return np.concatenate([cosine, cosine], 1), np.concatenate([-sine, sine], 1)


def bit_count(mask):
    mask = mask - ((mask >> 1) & 0x55555555)
    mask = (mask & 0x33333333) + ((mask >> 2) & 0x33333333)
    mask = (mask + (mask >> 4)) & 0x0F0F0F0F
    return (mask * 0x01010101) >> 24


def plan_kernel(peers, per_device, ancestors, grid, count, picks, ranks):
    d = lax.axis_index("dom")
    shape = grid.shape
    flat = lax.broadcasted_iota(jnp.int32, shape, 0) * shape[1] + lax.broadcasted_iota(
        jnp.int32, shape, 1
    )
    home = flat // per_device
    offset = grid[...] - next_chip(home) * per_device
    inside = (offset >= 0) & (offset < per_device)
    bits = jnp.where(inside, jnp.int32(1) << (offset & (per_device - 1)), 0)
    shift = 1
    while shift < per_device:
        bits = bits | pltpu.roll(bits, shape[1] - shift, 1)
        shift *= 2
    most = jnp.where(flat % per_device == 0, bit_count(bits), 0)
    count[0] = jnp.max(most.astype(jnp.float32)).astype(jnp.int32)

    def needed(home, owner):
        mask = jnp.int32(0)
        for k in range(per_device):
            offset = ancestors[home * per_device + k] - owner * per_device
            inside = (offset >= 0) & (offset < per_device)
            mask = mask | jnp.where(inside, jnp.int32(1) << (offset & (per_device - 1)), 0)
        return mask

    there = next_chip(d)
    mask = needed(jnp.clip(there, 0, peers - 1), d)
    position = jnp.int32(0)
    for j in range(per_device):
        picks[j] = 0
    for j in range(per_device):
        picks[position] = j
        position = position + ((mask >> j) & 1)
    mask = needed(d, there)
    for k in range(per_device):
        offset = ancestors[d * per_device + k] - there * per_device
        inside = (offset >= 0) & (offset < per_device)
        below = (jnp.int32(1) << (offset & (per_device - 1))) - 1
        ranks[k] = jnp.where(inside, bit_count(mask & below), -1)


def plan(ancestors, peers, per_device):
    return pl.pallas_call(
        functools.partial(plan_kernel, peers, per_device),
        out_shape=(
            jax.ShapeDtypeStruct((1,), jnp.int32),
            jax.ShapeDtypeStruct((per_device,), jnp.int32),
            jax.ShapeDtypeStruct((per_device,), jnp.int32),
        ),
        in_specs=[SMEM, VMEM],
        out_specs=(SMEM, SMEM, SMEM),
        cost_estimate=LIGHT,
        name="plan",
    )(ancestors, ancestors.reshape(-1, 128))


def gather_kernel(skip, size, picks, cache, sent, sems):
    def load(i, c):
        return pltpu.make_async_copy(cache.at[c, picks[skip + i]], sent.at[c, i], sems.at[c, i])

    def each(act):
        def body(i, carry):
            for c in range(2):
                act(load(i, c))
            return carry

        lax.fori_loop(0, size, body, 0)

    each(lambda copy: copy.start())
    each(lambda copy: copy.wait())


def gather(picks, cache, skip, size):
    shape = (2, size, *cache.shape[2:])
    return pl.pallas_call(
        functools.partial(gather_kernel, skip, size),
        out_shape=pltpu.VMEM(shape, cache.dtype),
        in_specs=[SMEM, HBM],
        out_specs=VMEM,
        scratch_shapes=[pltpu.SemaphoreType.DMA((2, size))],
        compiler_params=pltpu.CompilerParams(vmem_limit_bytes=12 * 2**20),
        cost_estimate=LIGHT,
        name="gather",
    )(picks, cache)


def place_kernel(per_device, find, tables, *refs):
    numbers, refs = refs[:tables], refs[tables:]
    *sources, _, out, held, loads, stores = refs
    d = lax.axis_index("dom")

    def each(act):
        def body(k, carry):
            for source, (there, at) in zip(sources, find(numbers, d, k)):

                @pl.when(there)
                def _():
                    for c in range(2):
                        act(source, at, k, c)

            return carry

        lax.fori_loop(0, per_device, body, 0)

    def load(source, at, k, c):
        return pltpu.make_async_copy(source.at[c, at], held.at[c, k], loads.at[c, k])

    def store(k, c):
        return pltpu.make_async_copy(held.at[c, k], out.at[c, k], stores.at[c, k])

    def forward(source, at, k, c):
        load(source, at, k, c).wait()
        store(k, c).start()

    each(lambda source, at, k, c: load(source, at, k, c).start())
    each(forward)
    each(lambda source, at, k, c: store(k, c).wait())


def place(find, numbers, sources, placed, name):
    per_device = placed.shape[1]
    operands = [*numbers, *sources, placed]
    return pl.pallas_call(
        functools.partial(place_kernel, per_device, find, len(numbers)),
        out_shape=pltpu.HBM(placed.shape, placed.dtype),
        in_specs=[SMEM] * len(numbers) + [ANY] * len(sources) + [HBM],
        out_specs=HBM,
        scratch_shapes=[
            pltpu.VMEM(placed.shape, placed.dtype),
            pltpu.SemaphoreType.DMA((2, per_device)),
            pltpu.SemaphoreType.DMA((2, per_device)),
        ],
        input_output_aliases={len(operands) - 1: 0},
        compiler_params=pltpu.CompilerParams(vmem_limit_bytes=12 * 2**20),
        cost_estimate=LIGHT,
        name=name,
    )(*operands)


def place_first(ancestors, ranks, mate, came, placed):
    per_device, size = placed.shape[1], came.shape[1]

    def find(numbers, d, k):
        ancestors, ranks = numbers
        offset = ancestors[d * per_device + k] - chip_mate(d) * per_device
        yield (offset >= 0) & (offset < per_device), offset
        yield (ranks[k] >= 0) & (ranks[k] < size), ranks[k]

    return place(find, [ancestors, ranks], [mate, came], placed, "place_first")


def place_more(ranks, came, placed, skip):
    size = came.shape[1]

    def find(numbers, d, k):
        rank = numbers[0][k] - skip
        yield (rank >= 0) & (rank < size), rank

    return place(find, [ranks], [came], placed, "place_more")


def serve_kernel(
    peers, per_device, heads, groups,
    ancestors, parent_twist, log_ratio, twist_weight, own, mate, far, cosine, sine, wq, wk, wv, cache,
    keys, values, out_own, out_others, part, placed,
    held, weights_q, weights_k, weights_v, total, turned, tokens, fresh, results,
    lists, slots, owners, loads, stores, streams,
):
    d = lax.axis_index("dom")
    first_lane = (lax.axis_index("tp") == 0).astype(jnp.float32)
    tile = DECODE_STEPS * heads
    queries = per_device * tile
    small = per_device * DECODE_STEPS
    homes = (d, chip_mate(d), next_chip(d))
    width_q, width_k = heads * HEAD_SIZE, groups * HEAD_SIZE
    chunks = streams.shape[1]
    depth = wq.shape[0] // chunks

    def stream(i, k):
        rows = pl.ds(pl.multiple_of(k * depth, depth), depth)
        source, target = ((wq, weights_q), (wk, weights_k), (wv, weights_v))[i]
        return pltpu.make_async_copy(source.at[rows, :], target.at[rows, :], streams.at[i, k])

    def begin(k, carry):
        for i in range(3):
            stream(i, k).start()
        return carry

    lax.fori_loop(0, chunks, begin, 0)

    def load(j, c):
        return pltpu.make_async_copy(cache.at[c, j], held.at[c, j], loads.at[c, j])

    def clear(j, carry):
        lists[j] = -1
        return carry

    lax.fori_loop(0, per_device, clear, 0)
    for h, home in enumerate(homes):
        there = (home >= 0) & (home < peers)
        start = jnp.clip(home, 0, peers - 1) * per_device

        def enlist(k, carry):
            offset = ancestors[start + k] - d * per_device

            @pl.when(there & (offset >= 0) & (offset < per_device))
            def _():
                slot = h * per_device + k
                lists[per_device + slot] = lists[offset]
                lists[offset] = slot

            return carry

        lax.fori_loop(0, per_device, enlist, 0)

    def flatten(j, count):
        def step(state):
            slot, count = state
            slots[count] = slot
            owners[count] = j
            return lists[per_device + slot], count + 1

        return lax.while_loop(lambda state: state[0] >= 0, step, (lists[j], count))[1]

    count = lax.fori_loop(0, per_device, flatten, jnp.int32(0))
    for extra in range(AT_ONCE - 1):

        @pl.when(count > 0)
        def _():
            slots[count + extra] = slots[count - 1]
            owners[count + extra] = owners[count - 1]

    part[...] = jnp.zeros_like(part)
    part[3 * per_device :, :DECODE_STEPS] = log_ratio[...] * first_lane
    results[...] = jnp.zeros_like(results)
    total[...] = jnp.zeros_like(total)
    per_chunk = per_device // chunks

    def project(k, carry):
        for i in range(3):
            stream(i, k).wait()
        for j in range(per_chunk):
            for c in range(2):
                load(k * per_chunk + j, c).start()
        at = pl.ds(pl.multiple_of(k * depth, depth), depth)
        rows = jnp.concatenate([own[:, at], mate[:, at], far[:, at]], 0)
        lanes = 0
        for weight, width in ((weights_q, width_q), (weights_k, width_k), (weights_v, width_k)):
            total[:, lanes : lanes + width] += jnp.dot(
                rows, weight[at, :], preferred_element_type=jnp.float32
            )
            lanes += width
        return carry

    lax.fori_loop(0, chunks, project, 0)

    def turn(x):
        return x * cosine[...] + pltpu.roll(x, HEAD_SIZE // 2, 1) * sine[...]

    block = 2 * groups * small
    for h in range(3):
        mine = slice(h * small, (h + 1) * small)
        for i in range(heads):
            turned[:, i, :] = turn(total[mine, i * HEAD_SIZE : (i + 1) * HEAD_SIZE])
        tokens[h * queries : (h + 1) * queries, :] = (
            turned[...].reshape(queries, HEAD_SIZE).astype(tokens.dtype)
        )
        for g in range(groups):
            lanes = slice(g * HEAD_SIZE, (g + 1) * HEAD_SIZE)
            at = width_q + g * HEAD_SIZE
            key = turn(total[mine, at : at + HEAD_SIZE]).astype(keys.dtype)
            at = at + width_k
            value = total[mine, at : at + HEAD_SIZE].astype(values.dtype)
            at = h * block + g * small
            fresh[at : at + small, :] = key.astype(jnp.float32)
            at = at + groups * small
            fresh[at : at + small, :] = value.astype(jnp.float32)
            if h == 0:
                keys[:, lanes] = key
                values[:, lanes] = value

    row = lax.broadcasted_iota(jnp.int32, (tile, 1), 0)
    lower = (row % heads) < heads // groups
    later = row >= heads
    lane = lax.broadcasted_iota(jnp.int32, (1, HEAD_SIZE), 1)
    scale = 1.0 / math.sqrt(HEAD_SIZE)
    twist = jnp.concatenate([jnp.zeros_like(twist_weight), twist_weight[...]], 0)

    def by_group(at):
        pair = [fresh[pl.ds(at + g * small, 1), :] for g in range(groups)]
        return jnp.where(lower, pair[0], pair[1])

    def scores_of(j, slot):
        query = tokens[pl.ds(pl.multiple_of(slot * tile, tile), tile), :]
        none = jnp.zeros_like(query)
        wide = jnp.concatenate([jnp.where(lower, query, none), jnp.where(lower, none, query)], 1)
        scores = (
            lax.dot_general(
                wide, held[0, j], (((1,), (1,)), ((), ())), preferred_element_type=jnp.float32
            )
            * scale
        )
        return query.astype(jnp.float32), scores

    def weights_of(scores):
        maxima = jnp.max(scores, 1, keepdims=True)
        return maxima, jnp.exp(scores - maxima)

    def finish(j, slot, query, maxima, totals, both):
        weighted = jnp.where(lower, both[:, :HEAD_SIZE], both[:, HEAD_SIZE:])
        at = (slot // per_device) * block + (slot % per_device) * DECODE_STEPS
        new = [
            jnp.sum(query * by_group(at + u), 1, keepdims=True) * scale
            for u in range(DECODE_STEPS)
        ]
        new[1] = jnp.where(later, new[1], -jnp.inf)
        peak = jnp.maximum(maxima, jnp.maximum(new[0], new[1]))
        carried = jnp.exp(maxima - peak)
        numerator = carried * weighted
        denominator = carried * totals
        for u in range(DECODE_STEPS):
            share = jnp.exp(new[u] - peak)
            numerator = numerator + share * by_group(at + groups * small + u)
            denominator = denominator + share
        outputs = numerator / denominator
        results[pl.ds(pl.multiple_of(slot * tile, tile), tile), :] = outputs.astype(jnp.bfloat16)
        twisted = jnp.sum(outputs * twist, 0, keepdims=True)
        less = jnp.where(lane == 0, parent_twist[j] * first_lane, 0.0)
        part[pl.ds(slot, 1), :] = twisted - less

    def store(k, j, c):
        return pltpu.make_async_copy(held.at[c, j], placed.at[c, k], stores.at[c, k])

    def arrive(j, carry):
        for c in range(2):
            load(j, c).wait()

        def step(slot):
            @pl.when(slot < per_device)
            def _():
                for c in range(2):
                    store(slot, j, c).start()

            return lists[per_device + slot]

        lax.while_loop(lambda slot: slot >= 0, step, lists[j])
        return carry

    def serve(step, loaded):
        at = step * AT_ONCE
        last = owners[at + AT_ONCE - 1] + 1
        lax.fori_loop(loaded, last, arrive, 0)
        jobs = [(owners[at + i], slots[at + i]) for i in range(AT_ONCE)]
        scored = [scores_of(*job) for job in jobs]
        weights = [weights_of(scores) for _, scores in scored]
        totals = [jnp.sum(expo, 1, keepdims=True) for _, expo in weights]
        both = [
            jnp.dot(expo.astype(jnp.bfloat16), held[1, job[0]], preferred_element_type=jnp.float32)
            for job, (_, expo) in zip(jobs, weights)
        ]
        for i, job in enumerate(jobs):
            finish(*job, scored[i][0], weights[i][0], totals[i], both[i])
        return last

    loaded = lax.fori_loop(0, (count + AT_ONCE - 1) // AT_ONCE, serve, jnp.int32(0))
    lax.fori_loop(loaded, per_device, arrive, 0)
    out_own[...] = results[:queries, :]
    out_others[...] = results[queries:, :]

    def settle(k, carry):
        offset = ancestors[d * per_device + k] - d * per_device

        @pl.when((offset >= 0) & (offset < per_device))
        def _():
            for c in range(2):
                store(k, offset, c).wait()

        return carry

    lax.fori_loop(0, per_device, settle, 0)


def serve(ancestors, parent_twist, log_ratio, twist_weight, own, mate, far, wq, wk, wv, cache, peers):
    per_device, anchor_point = cache.shape[1:3]
    heads, groups = wq.shape[1] // HEAD_SIZE, wk.shape[1] // HEAD_SIZE
    tile = DECODE_STEPS * heads
    queries = per_device * tile
    small = per_device * DECODE_STEPS
    cosine, sine = rope_tables(small, anchor_point)
    columns = wq.shape[1] + wk.shape[1] + wv.shape[1]
    chunks = 8
    return pl.pallas_call(
        functools.partial(serve_kernel, peers, per_device, heads, groups),
        out_shape=(
            jax.ShapeDtypeStruct((small, groups * HEAD_SIZE), jnp.bfloat16),
            jax.ShapeDtypeStruct((small, groups * HEAD_SIZE), jnp.bfloat16),
            jax.ShapeDtypeStruct((queries, HEAD_SIZE), jnp.bfloat16),
            jax.ShapeDtypeStruct((2 * queries, HEAD_SIZE), jnp.bfloat16),
            jax.ShapeDtypeStruct((4 * per_device, HEAD_SIZE), jnp.float32),
            pltpu.HBM(cache.shape, cache.dtype),
        ),
        in_specs=[SMEM, SMEM] + [VMEM] * 7 + [HBM] * 4,
        out_specs=(VMEM, VMEM, VMEM, VMEM, VMEM, HBM),
        scratch_shapes=[
            pltpu.VMEM(cache.shape, cache.dtype),
            pltpu.VMEM(wq.shape, wq.dtype),
            pltpu.VMEM(wk.shape, wk.dtype),
            pltpu.VMEM(wv.shape, wv.dtype),
            pltpu.VMEM((3 * small, columns), jnp.float32),
            pltpu.VMEM((small, heads, HEAD_SIZE), jnp.float32),
            pltpu.VMEM((3 * queries, HEAD_SIZE), jnp.bfloat16),
            pltpu.VMEM((3 * 2 * groups * small, HEAD_SIZE), jnp.float32),
            pltpu.VMEM((3 * queries, HEAD_SIZE), jnp.bfloat16),
            pltpu.SMEM((4 * per_device,), jnp.int32),
            pltpu.SMEM((3 * per_device + AT_ONCE,), jnp.int32),
            pltpu.SMEM((3 * per_device + AT_ONCE,), jnp.int32),
            pltpu.SemaphoreType.DMA((2, per_device)),
            pltpu.SemaphoreType.DMA((2, per_device)),
            pltpu.SemaphoreType.DMA((3, chunks)),
        ],
        compiler_params=pltpu.CompilerParams(vmem_limit_bytes=59 * 2**20),
        cost_estimate=LIGHT,
        name="serve",
    )(ancestors, parent_twist, log_ratio, twist_weight, own, mate, far, cosine, sine, wq, wk, wv, cache)


def normalise_kernel(terms, *refs):
    *parts, out = refs
    del terms
    total = parts[0][...]
    for part in parts[1:]:
        total = total + part[...]
    peak = jnp.max(total, keepdims=True)
    mass = jnp.sum(jnp.exp(total - peak), keepdims=True)
    row = lax.broadcasted_iota(jnp.int32, total.shape, 0)
    mine = jnp.sum(jnp.where(row == lax.axis_index("dom"), total, 0.0), 0, keepdims=True)
    out[...] = mine - (peak + jnp.log(mass))


def normalise(parts):
    return pl.pallas_call(
        functools.partial(normalise_kernel, len(parts)),
        out_shape=jax.ShapeDtypeStruct((1, parts[0].shape[1]), jnp.float32),
        in_specs=[VMEM] * len(parts),
        out_specs=VMEM,
        compiler_params=SMALL,
        cost_estimate=LIGHT,
        name="normalise",
    )(*parts)


def total_but_y(x, peers):
    side = math.isqrt(peers // 2)
    on_chip = [(i, i ^ 1) for i in range(peers)]
    x = x + lax.ppermute(x, "dom", on_chip)
    ring, hop = lax.axis_size("tp"), 1
    while hop < ring:
        x = x + lax.ppermute(x, "tp", [(i, i ^ hop) for i in range(ring)])
        hop *= 2
    step = 2 * side
    pairs = [(i, (i + step * (1 - 2 * (i % 2))) % peers) for i in range(peers)]
    first = lax.ppermute(x, "dom", pairs)
    return x + first + lax.ppermute(first, "dom", pairs) + lax.ppermute(first, "dom", on_chip)


def parts_along_y(x, peers):
    step = 2 * math.isqrt(peers // 2)
    parts = [x]
    for hop in range(2, step, 2):
        pairs = [(i, i // step * step + (i + hop) % step) for i in range(peers)]
        parts.append(lax.ppermute(x, "dom", pairs))
    return parts


def shards(
    cache,
    hidden,
    query_weight,
    key_projection_weight,
    value_projection_weight,
    twist_weight,
    parent_twist,
    log_ratio,
    ancestors,
):
    per_device = hidden.shape[0]
    heads = query_weight.shape[1] // HEAD_SIZE
    groups = key_projection_weight.shape[1] // HEAD_SIZE
    peers = lax.axis_size("dom")
    d = lax.axis_index("dom")
    on_chip = [(i, i ^ 1) for i in range(peers)]
    off_chip = [(i, i - 1 + 2 * (i % 2)) for i in range(1, peers - 1)]
    beside = [(i, i + 2 - 4 * (i % 2)) for i in range(peers) if 0 <= i + 2 - 4 * (i % 2) < peers]
    rows = hidden.reshape(per_device * DECODE_STEPS, -1)
    far_rows = lax.ppermute(rows, "dom", off_chip)
    mate_rows = lax.ppermute(rows, "dom", on_chip)
    count, picks, ranks = plan(ancestors, peers, per_device)
    came, skip = [], 0
    for size in PIECES:
        sent = gather(picks, cache, skip, size)
        if not came:
            sent, far_rows = lax.optimization_barrier((sent, far_rows))
        sent, picks = lax.optimization_barrier((sent, picks))
        came.append(lax.ppermute(sent, "dom", off_chip))
        skip += size
    late_cache, far_rows, mate_rows = lax.optimization_barrier((cache, far_rows, mate_rows))
    mate_cache = lax.ppermute(late_cache, "dom", on_chip)
    keys, values, own_part, others_part, part, out = serve(
        ancestors, parent_twist, log_ratio, twist_weight.reshape(heads, HEAD_SIZE),
        rows, mate_rows, far_rows, query_weight, key_projection_weight, value_projection_weight,
        cache, peers,
    )
    part = jnp.sum(part, 1).reshape(4, per_device)
    index = jnp.arange(peers)[:, None]
    spread = jnp.where(
        index == d,
        part[0] + part[3],
        jnp.where(index == chip_mate(d), part[1], jnp.where(index == next_chip(d), part[2], 0.0)),
    )
    spread = total_but_y(spread, peers)
    mate_part, far_part = jnp.split(lax.ppermute(others_part, "dom", on_chip), 2)
    far_part = lax.ppermute(far_part, "dom", beside)
    owner = lax.dynamic_slice_in_dim(ancestors, d * per_device, per_device) // per_device
    owner = jnp.repeat(owner, DECODE_STEPS * heads)[:, None]
    attention = jnp.where(
        owner == d, own_part, jnp.where(owner == chip_mate(d), mate_part, far_part)
    ).reshape(per_device, DECODE_STEPS, heads * HEAD_SIZE)
    out = place_first(ancestors, ranks, mate_cache, came[0], out)
    spread, out = lax.optimization_barrier((spread, out))
    log_weights = normalise(parts_along_y(spread, peers)).reshape(per_device)
    fresh = jnp.stack([keys, values]).reshape(2, per_device, DECODE_STEPS, groups * HEAD_SIZE)

    def more(size):
        def branch(cache, picks, ranks, out):
            came = lax.ppermute(gather(picks, cache, ALWAYS, size), "dom", off_chip)
            return place_more(ranks, came, out, ALWAYS)

        return branch

    out = lax.switch(
        jnp.maximum(count[0] - ALWAYS, 0),
        [lambda cache, picks, ranks, out: out] + [more(i + 1) for i in range(per_device - ALWAYS)],
        cache, picks, ranks, out,
    )
    skip = PIECES[0]
    for piece in came[1:]:
        out = place_more(ranks, piece, out, skip)
        skip += piece.shape[1]
    return (out, fresh, attention, log_weights)


def solution(mesh):
    return jax.shard_map(
        shards,
        mesh=mesh,
        in_specs=(
            P(None, "dom", None, "tp"),
            P("dom", None, None),
            P(None, "tp"),
            P(None, "tp"),
            P(None, "tp"),
            P("tp"),
            P("dom"),
            P("dom", None),
            P(),
        ),
        out_specs=(
            P(None, "dom", None, "tp"),
            P(None, "dom", None, "tp"),
            P("dom", None, "tp"),
            P("dom"),
        ),
        check_vma=False,
    )
```

```python
import functools
import math

import jax
import jax.numpy as jnp
import numpy as np
from jax import lax
from jax.experimental import pallas as pl
from jax.experimental.pallas import tpu as pltpu
from jax.sharding import PartitionSpec as P

HEAD_SIZE = 128
DECODE_STEPS = 2
ROPE_BASE = 500000.0
PIECES = (6, 2)
ALWAYS = sum(PIECES)
AT_ONCE = 4

SMEM = pl.BlockSpec(memory_space=pltpu.SMEM)
VMEM = pl.BlockSpec(memory_space=pltpu.VMEM)
ANY = pl.BlockSpec(memory_space=pl.ANY)
HBM = pl.BlockSpec(memory_space=pltpu.HBM)
SMALL = pltpu.CompilerParams(vmem_limit_bytes=2 * 2**20)
LIGHT = pl.CostEstimate(flops=0, bytes_accessed=0, transcendentals=0)


def chip_mate(d):
    return d + 1 - 2 * (d % 2)


def next_chip(d):
    return d - 1 + 2 * (d % 2)


def rope_tables(rows, anchor_point):
    half = HEAD_SIZE // 2
    frequency = np.exp(
        np.arange(half, dtype=np.float32) * np.float32(-2.0 * math.log(ROPE_BASE) / HEAD_SIZE)
    ).astype(np.float32)
    positions = (anchor_point + np.arange(rows) % DECODE_STEPS).astype(np.float32)
    angles = (positions[:, None] * frequency[None, :]).astype(np.float32)
    cosine = np.cos(angles).astype(np.float32)
    sine = np.sin(angles).astype(np.float32)
    return np.concatenate([cosine, cosine], 1), np.concatenate([-sine, sine], 1)


def bit_count(mask):
    mask = mask - ((mask >> 1) & 0x55555555)
    mask = (mask & 0x33333333) + ((mask >> 2) & 0x33333333)
    mask = (mask + (mask >> 4)) & 0x0F0F0F0F
    return (mask * 0x01010101) >> 24


def plan_kernel(peers, per_device, ancestors, grid, count, picks, ranks):
    d = lax.axis_index("dom")
    shape = grid.shape
    flat = lax.broadcasted_iota(jnp.int32, shape, 0) * shape[1] + lax.broadcasted_iota(
        jnp.int32, shape, 1
    )
    home = flat // per_device
    offset = grid[...] - next_chip(home) * per_device
    inside = (offset >= 0) & (offset < per_device)
    bits = jnp.where(inside, jnp.int32(1) << (offset & (per_device - 1)), 0)
    shift = 1
    while shift < per_device:
        bits = bits | pltpu.roll(bits, shape[1] - shift, 1)
        shift *= 2
    most = jnp.where(flat % per_device == 0, bit_count(bits), 0)
    count[0] = jnp.max(most.astype(jnp.float32)).astype(jnp.int32)

    def needed(home, owner):
        mask = jnp.int32(0)
        for k in range(per_device):
            offset = ancestors[home * per_device + k] - owner * per_device
            inside = (offset >= 0) & (offset < per_device)
            mask = mask | jnp.where(inside, jnp.int32(1) << (offset & (per_device - 1)), 0)
        return mask

    there = next_chip(d)
    mask = needed(jnp.clip(there, 0, peers - 1), d)
    position = jnp.int32(0)
    for j in range(per_device):
        picks[j] = 0
    for j in range(per_device):
        picks[position] = j
        position = position + ((mask >> j) & 1)
    mask = needed(d, there)
    for k in range(per_device):
        offset = ancestors[d * per_device + k] - there * per_device
        inside = (offset >= 0) & (offset < per_device)
        below = (jnp.int32(1) << (offset & (per_device - 1))) - 1
        ranks[k] = jnp.where(inside, bit_count(mask & below), -1)


def plan(ancestors, peers, per_device):
    return pl.pallas_call(
        functools.partial(plan_kernel, peers, per_device),
        out_shape=(
            jax.ShapeDtypeStruct((1,), jnp.int32),
            jax.ShapeDtypeStruct((per_device,), jnp.int32),
            jax.ShapeDtypeStruct((per_device,), jnp.int32),
        ),
        in_specs=[SMEM, VMEM],
        out_specs=(SMEM, SMEM, SMEM),
        cost_estimate=LIGHT,
        name="plan",
    )(ancestors, ancestors.reshape(-1, 128))


def gather_kernel(skip, size, picks, cache, sent, sems):
    def load(i, c):
        return pltpu.make_async_copy(cache.at[c, picks[skip + i]], sent.at[c, i], sems.at[c, i])

    def each(act):
        def body(i, carry):
            for c in range(2):
                act(load(i, c))
            return carry

        lax.fori_loop(0, size, body, 0)

    each(lambda copy: copy.start())
    each(lambda copy: copy.wait())


def gather(picks, cache, skip, size):
    shape = (2, size, *cache.shape[2:])
    return pl.pallas_call(
        functools.partial(gather_kernel, skip, size),
        out_shape=pltpu.VMEM(shape, cache.dtype),
        in_specs=[SMEM, HBM],
        out_specs=VMEM,
        scratch_shapes=[pltpu.SemaphoreType.DMA((2, size))],
        compiler_params=pltpu.CompilerParams(vmem_limit_bytes=12 * 2**20),
        cost_estimate=LIGHT,
        name="gather",
    )(picks, cache)


def place_kernel(per_device, find, tables, *refs):
    numbers, refs = refs[:tables], refs[tables:]
    *sources, _, out, held, loads, stores = refs
    d = lax.axis_index("dom")

    def each(act):
        def body(k, carry):
            for source, (there, at) in zip(sources, find(numbers, d, k)):

                @pl.when(there)
                def _():
                    for c in range(2):
                        act(source, at, k, c)

            return carry

        lax.fori_loop(0, per_device, body, 0)

    def load(source, at, k, c):
        return pltpu.make_async_copy(source.at[c, at], held.at[c, k], loads.at[c, k])

    def store(k, c):
        return pltpu.make_async_copy(held.at[c, k], out.at[c, k], stores.at[c, k])

    def forward(source, at, k, c):
        load(source, at, k, c).wait()
        store(k, c).start()

    each(lambda source, at, k, c: load(source, at, k, c).start())
    each(forward)
    each(lambda source, at, k, c: store(k, c).wait())


def place(find, numbers, sources, placed, name):
    per_device = placed.shape[1]
    operands = [*numbers, *sources, placed]
    return pl.pallas_call(
        functools.partial(place_kernel, per_device, find, len(numbers)),
        out_shape=pltpu.HBM(placed.shape, placed.dtype),
        in_specs=[SMEM] * len(numbers) + [ANY] * len(sources) + [HBM],
        out_specs=HBM,
        scratch_shapes=[
            pltpu.VMEM(placed.shape, placed.dtype),
            pltpu.SemaphoreType.DMA((2, per_device)),
            pltpu.SemaphoreType.DMA((2, per_device)),
        ],
        input_output_aliases={len(operands) - 1: 0},
        compiler_params=pltpu.CompilerParams(vmem_limit_bytes=12 * 2**20),
        cost_estimate=LIGHT,
        name=name,
    )(*operands)


def place_first(ancestors, ranks, mate, came, placed):
    per_device, size = placed.shape[1], came.shape[1]

    def find(numbers, d, k):
        ancestors, ranks = numbers
        offset = ancestors[d * per_device + k] - chip_mate(d) * per_device
        yield (offset >= 0) & (offset < per_device), offset
        yield (ranks[k] >= 0) & (ranks[k] < size), ranks[k]

    return place(find, [ancestors, ranks], [mate, came], placed, "place_first")


def place_more(ranks, came, placed, skip):
    size = came.shape[1]

    def find(numbers, d, k):
        rank = numbers[0][k] - skip
        yield (rank >= 0) & (rank < size), rank

    return place(find, [ranks], [came], placed, "place_more")


def serve_kernel(
    peers, per_device, heads, groups,
    ancestors, picks, parent_twist, log_ratio, twist_weight, own, mate, far, cosine, sine,
    wq, wk, wv, cache,
    keys, values, out_own, out_others, spread, placed, sent,
    held, weights_q, weights_k, weights_v, total, turned, tokens, fresh, results,
    part, lists, slots, owners, loads, stores, streams, sends,
):
    d = lax.axis_index("dom")
    first_lane = (lax.axis_index("tp") == 0).astype(jnp.float32)
    tile = DECODE_STEPS * heads
    queries = per_device * tile
    small = per_device * DECODE_STEPS
    homes = (d, chip_mate(d), next_chip(d))
    width_q, width_k = heads * HEAD_SIZE, groups * HEAD_SIZE
    chunks = streams.shape[1]
    depth = wq.shape[0] // chunks

    def stream(i, k):
        rows = pl.ds(pl.multiple_of(k * depth, depth), depth)
        source, target = ((wq, weights_q), (wk, weights_k), (wv, weights_v))[i]
        return pltpu.make_async_copy(source.at[rows, :], target.at[rows, :], streams.at[i, k])

    def begin(k, carry):
        for i in range(3):
            stream(i, k).start()
        return carry

    lax.fori_loop(0, chunks, begin, 0)

    def load(j, c):
        return pltpu.make_async_copy(cache.at[c, j], held.at[c, j], loads.at[c, j])

    def clear(j, carry):
        lists[j] = -1
        return carry

    lax.fori_loop(0, per_device, clear, 0)
    for h, home in enumerate(homes):
        there = (home >= 0) & (home < peers)
        start = jnp.clip(home, 0, peers - 1) * per_device

        def enlist(k, carry):
            offset = ancestors[start + k] - d * per_device

            @pl.when(there & (offset >= 0) & (offset < per_device))
            def _():
                slot = h * per_device + k
                lists[per_device + slot] = lists[offset]
                lists[offset] = slot

            return carry

        lax.fori_loop(0, per_device, enlist, 0)

    def flatten(j, count):
        def step(state):
            slot, count = state
            slots[count] = slot
            owners[count] = j
            return lists[per_device + slot], count + 1

        return lax.while_loop(lambda state: state[0] >= 0, step, (lists[j], count))[1]

    count = lax.fori_loop(0, per_device, flatten, jnp.int32(0))
    for extra in range(AT_ONCE - 1):

        @pl.when(count > 0)
        def _():
            slots[count + extra] = slots[count - 1]
            owners[count + extra] = owners[count - 1]

    part[...] = jnp.zeros_like(part)
    results[...] = jnp.zeros_like(results)
    total[...] = jnp.zeros_like(total)
    per_chunk = per_device // chunks

    def project(k, carry):
        for i in range(3):
            stream(i, k).wait()
        for j in range(per_chunk):
            for c in range(2):
                load(k * per_chunk + j, c).start()
        at = pl.ds(pl.multiple_of(k * depth, depth), depth)
        rows = jnp.concatenate([own[:, at], mate[:, at], far[:, at]], 0)
        lanes = 0
        for weight, width in ((weights_q, width_q), (weights_k, width_k), (weights_v, width_k)):
            total[:, lanes : lanes + width] += jnp.dot(
                rows, weight[at, :], preferred_element_type=jnp.float32
            )
            lanes += width
        return carry

    lax.fori_loop(0, chunks, project, 0)

    def turn(x):
        return x * cosine[...] + pltpu.roll(x, HEAD_SIZE // 2, 1) * sine[...]

    block = 2 * groups * small
    for h in range(3):
        mine = slice(h * small, (h + 1) * small)
        for i in range(heads):
            turned[:, i, :] = turn(total[mine, i * HEAD_SIZE : (i + 1) * HEAD_SIZE])
        tokens[h * queries : (h + 1) * queries, :] = (
            turned[...].reshape(queries, HEAD_SIZE).astype(tokens.dtype)
        )
        for g in range(groups):
            lanes = slice(g * HEAD_SIZE, (g + 1) * HEAD_SIZE)
            at = width_q + g * HEAD_SIZE
            key = turn(total[mine, at : at + HEAD_SIZE]).astype(keys.dtype)
            at = at + width_k
            value = total[mine, at : at + HEAD_SIZE].astype(values.dtype)
            at = h * block + g * small
            fresh[at : at + small, :] = key.astype(jnp.float32)
            at = at + groups * small
            fresh[at : at + small, :] = value.astype(jnp.float32)
            if h == 0:
                keys[:, lanes] = key
                values[:, lanes] = value

    row = lax.broadcasted_iota(jnp.int32, (tile, 1), 0)
    lower = (row % heads) < heads // groups
    later = row >= heads
    lane = lax.broadcasted_iota(jnp.int32, (1, HEAD_SIZE), 1)
    scale = 1.0 / math.sqrt(HEAD_SIZE)
    twist = jnp.concatenate([jnp.zeros_like(twist_weight), twist_weight[...]], 0)

    def by_group(at):
        pair = [fresh[pl.ds(at + g * small, 1), :] for g in range(groups)]
        return jnp.where(lower, pair[0], pair[1])

    def scores_of(j, slot):
        query = tokens[pl.ds(pl.multiple_of(slot * tile, tile), tile), :]
        none = jnp.zeros_like(query)
        wide = jnp.concatenate([jnp.where(lower, query, none), jnp.where(lower, none, query)], 1)
        scores = (
            lax.dot_general(
                wide, held[0, j], (((1,), (1,)), ((), ())), preferred_element_type=jnp.float32
            )
            * scale
        )
        return query.astype(jnp.float32), scores

    def weights_of(scores):
        maxima = jnp.max(scores, 1, keepdims=True)
        return maxima, jnp.exp(scores - maxima)

    def finish(j, slot, query, maxima, totals, both):
        weighted = jnp.where(lower, both[:, :HEAD_SIZE], both[:, HEAD_SIZE:])
        at = (slot // per_device) * block + (slot % per_device) * DECODE_STEPS
        new = [
            jnp.sum(query * by_group(at + u), 1, keepdims=True) * scale
            for u in range(DECODE_STEPS)
        ]
        new[1] = jnp.where(later, new[1], -jnp.inf)
        peak = jnp.maximum(maxima, jnp.maximum(new[0], new[1]))
        carried = jnp.exp(maxima - peak)
        numerator = carried * weighted
        denominator = carried * totals
        for u in range(DECODE_STEPS):
            share = jnp.exp(new[u] - peak)
            numerator = numerator + share * by_group(at + groups * small + u)
            denominator = denominator + share
        outputs = numerator / denominator
        results[pl.ds(pl.multiple_of(slot * tile, tile), tile), :] = outputs.astype(jnp.bfloat16)
        twisted = jnp.sum(outputs * twist, 0, keepdims=True)
        less = jnp.where(lane == 0, parent_twist[j] * first_lane, 0.0)
        part[pl.ds(slot, 1), :] = twisted - less

    def store(k, j, c):
        return pltpu.make_async_copy(held.at[c, j], placed.at[c, k], stores.at[c, k])

    def arrive(j, carry):
        for c in range(2):
            load(j, c).wait()

        def step(slot):
            @pl.when(slot < per_device)
            def _():
                for c in range(2):
                    store(slot, j, c).start()

            return lists[per_device + slot]

        lax.while_loop(lambda slot: slot >= 0, step, lists[j])
        return carry

    def serve(step, loaded):
        at = step * AT_ONCE
        last = owners[at + AT_ONCE - 1] + 1
        lax.fori_loop(loaded, last, arrive, 0)
        jobs = [(owners[at + i], slots[at + i]) for i in range(AT_ONCE)]
        scored = [scores_of(*job) for job in jobs]
        weights = [weights_of(scores) for _, scores in scored]
        totals = [jnp.sum(expo, 1, keepdims=True) for _, expo in weights]
        both = [
            jnp.dot(expo.astype(jnp.bfloat16), held[1, job[0]], preferred_element_type=jnp.float32)
            for job, (_, expo) in zip(jobs, weights)
        ]
        for i, job in enumerate(jobs):
            finish(*job, scored[i][0], weights[i][0], totals[i], both[i])
        return last

    loaded = lax.fori_loop(0, (count + AT_ONCE - 1) // AT_ONCE, serve, jnp.int32(0))
    lax.fori_loop(loaded, per_device, arrive, 0)
    skip = PIECES[0]
    copies = [
        pltpu.make_async_copy(held.at[c, picks[skip + i]], sent.at[c, i], sends.at[c, i])
        for i in range(sent.shape[1])
        for c in range(2)
    ]
    for copy in copies:
        copy.start()
    sums = jnp.sum(jnp.transpose(part[...]), 0, keepdims=True)
    spread[...] = jnp.zeros_like(spread)
    for h, home in enumerate(homes):
        share = sums[:, h * per_device : (h + 1) * per_device]
        if h == 0:
            share = share + jnp.sum(log_ratio[...], 0, keepdims=True) * first_lane

        @pl.when((home >= 0) & (home < peers))
        def _():
            spread[pl.ds(jnp.clip(home, 0, peers - 1), 1), :] = share

    out_own[...] = results[:queries, :]
    out_others[...] = results[queries:, :]

    def settle(k, carry):
        offset = ancestors[d * per_device + k] - d * per_device

        @pl.when((offset >= 0) & (offset < per_device))
        def _():
            for c in range(2):
                store(k, offset, c).wait()

        return carry

    lax.fori_loop(0, per_device, settle, 0)
    for copy in copies:
        copy.wait()


def serve(ancestors, picks, parent_twist, log_ratio, twist_weight, own, mate, far, wq, wk, wv, cache, peers):
    per_device, anchor_point = cache.shape[1:3]
    heads, groups = wq.shape[1] // HEAD_SIZE, wk.shape[1] // HEAD_SIZE
    tile = DECODE_STEPS * heads
    queries = per_device * tile
    small = per_device * DECODE_STEPS
    cosine, sine = rope_tables(small, anchor_point)
    columns = wq.shape[1] + wk.shape[1] + wv.shape[1]
    chunks = 8
    return pl.pallas_call(
        functools.partial(serve_kernel, peers, per_device, heads, groups),
        out_shape=(
            jax.ShapeDtypeStruct((small, groups * HEAD_SIZE), jnp.bfloat16),
            jax.ShapeDtypeStruct((small, groups * HEAD_SIZE), jnp.bfloat16),
            jax.ShapeDtypeStruct((queries, HEAD_SIZE), jnp.bfloat16),
            jax.ShapeDtypeStruct((2 * queries, HEAD_SIZE), jnp.bfloat16),
            jax.ShapeDtypeStruct((peers, per_device), jnp.float32),
            pltpu.HBM(cache.shape, cache.dtype),
            pltpu.HBM((2, PIECES[1], *cache.shape[2:]), cache.dtype),
        ),
        in_specs=[SMEM, SMEM, SMEM] + [VMEM] * 7 + [HBM] * 4,
        out_specs=(VMEM, VMEM, VMEM, VMEM, VMEM, HBM, HBM),
        scratch_shapes=[
            pltpu.VMEM(cache.shape, cache.dtype),
            pltpu.VMEM(wq.shape, wq.dtype),
            pltpu.VMEM(wk.shape, wk.dtype),
            pltpu.VMEM(wv.shape, wv.dtype),
            pltpu.VMEM((3 * small, columns), jnp.float32),
            pltpu.VMEM((small, heads, HEAD_SIZE), jnp.float32),
            pltpu.VMEM((3 * queries, HEAD_SIZE), jnp.bfloat16),
            pltpu.VMEM((3 * 2 * groups * small, HEAD_SIZE), jnp.float32),
            pltpu.VMEM((3 * queries, HEAD_SIZE), jnp.bfloat16),
            pltpu.VMEM((HEAD_SIZE, HEAD_SIZE), jnp.float32),
            pltpu.SMEM((4 * per_device,), jnp.int32),
            pltpu.SMEM((3 * per_device + AT_ONCE,), jnp.int32),
            pltpu.SMEM((3 * per_device + AT_ONCE,), jnp.int32),
            pltpu.SemaphoreType.DMA((2, per_device)),
            pltpu.SemaphoreType.DMA((2, per_device)),
            pltpu.SemaphoreType.DMA((3, chunks)),
            pltpu.SemaphoreType.DMA((2, PIECES[1])),
        ],
        compiler_params=pltpu.CompilerParams(vmem_limit_bytes=59 * 2**20),
        cost_estimate=LIGHT,
        name="serve",
    )(
        ancestors, picks, parent_twist, log_ratio, twist_weight, own, mate, far, cosine, sine,
        wq, wk, wv, cache,
    )


def normalise_kernel(terms, *refs):
    *parts, out = refs
    del terms
    total = parts[0][...]
    for part in parts[1:]:
        total = total + part[...]
    peak = jnp.max(total, keepdims=True)
    mass = jnp.sum(jnp.exp(total - peak), keepdims=True)
    row = lax.broadcasted_iota(jnp.int32, total.shape, 0)
    mine = jnp.sum(jnp.where(row == lax.axis_index("dom"), total, 0.0), 0, keepdims=True)
    out[...] = mine - (peak + jnp.log(mass))


def normalise(parts):
    return pl.pallas_call(
        functools.partial(normalise_kernel, len(parts)),
        out_shape=jax.ShapeDtypeStruct((1, parts[0].shape[1]), jnp.float32),
        in_specs=[VMEM] * len(parts),
        out_specs=VMEM,
        compiler_params=SMALL,
        cost_estimate=LIGHT,
        name="normalise",
    )(*parts)


def total_but_y(x, peers):
    side = math.isqrt(peers // 2)
    on_chip = [(i, i ^ 1) for i in range(peers)]
    x = x + lax.ppermute(x, "dom", on_chip)
    ring, hop = lax.axis_size("tp"), 1
    while hop < ring:
        x = x + lax.ppermute(x, "tp", [(i, i ^ hop) for i in range(ring)])
        hop *= 2
    step = 2 * side
    pairs = [(i, (i + step * (1 - 2 * (i % 2))) % peers) for i in range(peers)]
    first = lax.ppermute(x, "dom", pairs)
    return x + first + lax.ppermute(first, "dom", pairs) + lax.ppermute(first, "dom", on_chip)


def parts_along_y(x, peers):
    step = 2 * math.isqrt(peers // 2)
    parts = [x]
    for hop in range(2, step, 2):
        pairs = [(i, i // step * step + (i + hop) % step) for i in range(peers)]
        parts.append(lax.ppermute(x, "dom", pairs))
    return parts


def shards(
    cache,
    hidden,
    query_weight,
    key_projection_weight,
    value_projection_weight,
    twist_weight,
    parent_twist,
    log_ratio,
    ancestors,
):
    per_device = hidden.shape[0]
    heads = query_weight.shape[1] // HEAD_SIZE
    groups = key_projection_weight.shape[1] // HEAD_SIZE
    peers = lax.axis_size("dom")
    d = lax.axis_index("dom")
    on_chip = [(i, i ^ 1) for i in range(peers)]
    off_chip = [(i, i - 1 + 2 * (i % 2)) for i in range(1, peers - 1)]
    beside = [(i, i + 2 - 4 * (i % 2)) for i in range(peers) if 0 <= i + 2 - 4 * (i % 2) < peers]
    rows = hidden.reshape(per_device * DECODE_STEPS, -1)
    far_rows = lax.ppermute(rows, "dom", off_chip)
    mate_rows = lax.ppermute(rows, "dom", on_chip)
    count, picks, ranks = plan(ancestors, peers, per_device)
    sent, far_rows = lax.optimization_barrier((gather(picks, cache, 0, PIECES[0]), far_rows))
    first = lax.ppermute(sent, "dom", off_chip)
    late_cache, far_rows, mate_rows = lax.optimization_barrier((cache, far_rows, mate_rows))
    mate_cache = lax.ppermute(late_cache, "dom", on_chip)
    keys, values, own_part, others_part, spread, out, sent = serve(
        ancestors, picks, parent_twist, log_ratio.T, twist_weight.reshape(heads, HEAD_SIZE),
        rows, mate_rows, far_rows, query_weight, key_projection_weight, value_projection_weight,
        cache, peers,
    )
    second = lax.ppermute(sent, "dom", off_chip)
    spread = total_but_y(spread, peers)
    mate_part, far_part = jnp.split(lax.ppermute(others_part, "dom", on_chip), 2)
    far_part = lax.ppermute(far_part, "dom", beside)
    owner = lax.dynamic_slice_in_dim(ancestors, d * per_device, per_device) // per_device
    owner = jnp.repeat(owner, DECODE_STEPS * heads)[:, None]
    attention = jnp.where(
        owner == d, own_part, jnp.where(owner == chip_mate(d), mate_part, far_part)
    ).reshape(per_device, DECODE_STEPS, heads * HEAD_SIZE)
    out = place_first(ancestors, ranks, mate_cache, first, out)
    spread, out = lax.optimization_barrier((spread, out))
    log_weights = normalise(parts_along_y(spread, peers)).reshape(per_device)
    fresh = jnp.stack([keys, values]).reshape(2, per_device, DECODE_STEPS, groups * HEAD_SIZE)

    def more(size):
        def branch(cache, picks, ranks, out):
            came = lax.ppermute(gather(picks, cache, ALWAYS, size), "dom", off_chip)
            return place_more(ranks, came, out, ALWAYS)

        return branch

    out = lax.switch(
        jnp.maximum(count[0] - ALWAYS, 0),
        [lambda cache, picks, ranks, out: out] + [more(i + 1) for i in range(per_device - ALWAYS)],
        cache, picks, ranks, out,
    )
    out = place_more(ranks, second, out, PIECES[0])
    return (out, fresh, attention, log_weights)


def solution(mesh):
    return jax.shard_map(
        shards,
        mesh=mesh,
        in_specs=(
            P(None, "dom", None, "tp"),
            P("dom", None, None),
            P(None, "tp"),
            P(None, "tp"),
            P(None, "tp"),
            P("tp"),
            P("dom"),
            P("dom", None),
            P(),
        ),
        out_specs=(
            P(None, "dom", None, "tp"),
            P(None, "dom", None, "tp"),
            P("dom", None, "tp"),
            P("dom"),
        ),
        check_vma=False,
    )
```

```python
import functools
import math

import jax
import jax.numpy as jnp
import numpy as np
from jax import lax
from jax.experimental import pallas as pl
from jax.experimental.pallas import tpu as pltpu
from jax.sharding import PartitionSpec as P

HEAD_SIZE = 128
DECODE_STEPS = 2
ROPE_BASE = 500000.0
PIECES = (6, 2)
ALWAYS = sum(PIECES)
AT_ONCE = 4

SMEM = pl.BlockSpec(memory_space=pltpu.SMEM)
VMEM = pl.BlockSpec(memory_space=pltpu.VMEM)
ANY = pl.BlockSpec(memory_space=pl.ANY)
HBM = pl.BlockSpec(memory_space=pltpu.HBM)
SMALL = pltpu.CompilerParams(vmem_limit_bytes=2 * 2**20)
LIGHT = pl.CostEstimate(flops=0, bytes_accessed=0, transcendentals=0)


def chip_mate(d):
    return d + 1 - 2 * (d % 2)


def next_chip(d):
    return d - 1 + 2 * (d % 2)


def rope_tables(rows, anchor_point):
    half = HEAD_SIZE // 2
    frequency = np.exp(
        np.arange(half, dtype=np.float32) * np.float32(-2.0 * math.log(ROPE_BASE) / HEAD_SIZE)
    ).astype(np.float32)
    positions = (anchor_point + np.arange(rows) % DECODE_STEPS).astype(np.float32)
    angles = (positions[:, None] * frequency[None, :]).astype(np.float32)
    cosine = np.cos(angles).astype(np.float32)
    sine = np.sin(angles).astype(np.float32)
    return np.concatenate([cosine, cosine], 1), np.concatenate([-sine, sine], 1)


def bit_count(mask):
    mask = mask - ((mask >> 1) & 0x55555555)
    mask = (mask & 0x33333333) + ((mask >> 2) & 0x33333333)
    mask = (mask + (mask >> 4)) & 0x0F0F0F0F
    return (mask * 0x01010101) >> 24


def plan_kernel(peers, per_device, ancestors, grid, count, picks, ranks):
    d = lax.axis_index("dom")
    shape = grid.shape
    flat = lax.broadcasted_iota(jnp.int32, shape, 0) * shape[1] + lax.broadcasted_iota(
        jnp.int32, shape, 1
    )
    home = flat // per_device
    offset = grid[...] - next_chip(home) * per_device
    inside = (offset >= 0) & (offset < per_device)
    bits = jnp.where(inside, jnp.int32(1) << (offset & (per_device - 1)), 0)
    shift = 1
    while shift < per_device:
        bits = bits | pltpu.roll(bits, shape[1] - shift, 1)
        shift *= 2
    most = jnp.where(flat % per_device == 0, bit_count(bits), 0)
    count[0] = jnp.max(most.astype(jnp.float32)).astype(jnp.int32)

    def needed(home, owner):
        mask = jnp.int32(0)
        for k in range(per_device):
            offset = ancestors[home * per_device + k] - owner * per_device
            inside = (offset >= 0) & (offset < per_device)
            mask = mask | jnp.where(inside, jnp.int32(1) << (offset & (per_device - 1)), 0)
        return mask

    there = next_chip(d)
    mask = needed(jnp.clip(there, 0, peers - 1), d)
    position = jnp.int32(0)
    for j in range(per_device):
        picks[j] = 0
    for j in range(per_device):
        picks[position] = j
        position = position + ((mask >> j) & 1)
    mask = needed(d, there)
    for k in range(per_device):
        offset = ancestors[d * per_device + k] - there * per_device
        inside = (offset >= 0) & (offset < per_device)
        below = (jnp.int32(1) << (offset & (per_device - 1))) - 1
        ranks[k] = jnp.where(inside, bit_count(mask & below), -1)


def plan(ancestors, peers, per_device):
    return pl.pallas_call(
        functools.partial(plan_kernel, peers, per_device),
        out_shape=(
            jax.ShapeDtypeStruct((1,), jnp.int32),
            jax.ShapeDtypeStruct((per_device,), jnp.int32),
            jax.ShapeDtypeStruct((per_device,), jnp.int32),
        ),
        in_specs=[SMEM, VMEM],
        out_specs=(SMEM, SMEM, SMEM),
        compiler_params=SMALL,
        cost_estimate=LIGHT,
        name="plan",
    )(ancestors, ancestors.reshape(-1, 128))


def gather_kernel(skip, size, picks, cache, sent, sems):
    def load(i, c):
        return pltpu.make_async_copy(cache.at[c, picks[skip + i]], sent.at[c, i], sems.at[c, i])

    def each(act):
        def body(i, carry):
            for c in range(2):
                act(load(i, c))
            return carry

        lax.fori_loop(0, size, body, 0)

    each(lambda copy: copy.start())
    each(lambda copy: copy.wait())


def gather(picks, cache, skip, size):
    shape = (2, size, *cache.shape[2:])
    return pl.pallas_call(
        functools.partial(gather_kernel, skip, size),
        out_shape=pltpu.VMEM(shape, cache.dtype),
        in_specs=[SMEM, HBM],
        out_specs=VMEM,
        scratch_shapes=[pltpu.SemaphoreType.DMA((2, size))],
        compiler_params=pltpu.CompilerParams(vmem_limit_bytes=12 * 2**20),
        cost_estimate=LIGHT,
        name="gather",
    )(picks, cache)


def place_kernel(per_device, find, tables, *refs):
    numbers, refs = refs[:tables], refs[tables:]
    *sources, _, out, held, loads, stores = refs
    d = lax.axis_index("dom")

    def each(act):
        def body(k, carry):
            for source, (there, at) in zip(sources, find(numbers, d, k)):

                @pl.when(there)
                def _():
                    for c in range(2):
                        act(source, at, k, c)

            return carry

        lax.fori_loop(0, per_device, body, 0)

    def load(source, at, k, c):
        return pltpu.make_async_copy(source.at[c, at], held.at[c, k], loads.at[c, k])

    def store(k, c):
        return pltpu.make_async_copy(held.at[c, k], out.at[c, k], stores.at[c, k])

    def forward(source, at, k, c):
        load(source, at, k, c).wait()
        store(k, c).start()

    each(lambda source, at, k, c: load(source, at, k, c).start())
    each(forward)
    each(lambda source, at, k, c: store(k, c).wait())


def place(find, numbers, sources, placed, name):
    per_device = placed.shape[1]
    operands = [*numbers, *sources, placed]
    return pl.pallas_call(
        functools.partial(place_kernel, per_device, find, len(numbers)),
        out_shape=pltpu.HBM(placed.shape, placed.dtype),
        in_specs=[SMEM] * len(numbers) + [ANY] * len(sources) + [HBM],
        out_specs=HBM,
        scratch_shapes=[
            pltpu.VMEM(placed.shape, placed.dtype),
            pltpu.SemaphoreType.DMA((2, per_device)),
            pltpu.SemaphoreType.DMA((2, per_device)),
        ],
        input_output_aliases={len(operands) - 1: 0},
        compiler_params=pltpu.CompilerParams(vmem_limit_bytes=12 * 2**20),
        cost_estimate=LIGHT,
        name=name,
    )(*operands)


def place_first(ancestors, ranks, mate, came, placed):
    per_device, size = placed.shape[1], came.shape[1]

    def find(numbers, d, k):
        ancestors, ranks = numbers
        offset = ancestors[d * per_device + k] - chip_mate(d) * per_device
        yield (offset >= 0) & (offset < per_device), offset
        yield (ranks[k] >= 0) & (ranks[k] < size), ranks[k]

    return place(find, [ancestors, ranks], [mate, came], placed, "place_first")


def place_more(ranks, came, placed, skip):
    size = came.shape[1]

    def find(numbers, d, k):
        rank = numbers[0][k] - skip
        yield (rank >= 0) & (rank < size), rank

    return place(find, [ranks], [came], placed, "place_more")


def serve_kernel(
    peers, per_device, heads, groups,
    ancestors, picks, parent_twist, log_ratio, twist_weight, own, mate, far, cosine, sine,
    wq, wk, wv, cache,
    keys, values, out_own, out_others, spread, placed, sent,
    held, total, turned, tokens, fresh, results,
    part, lists, slots, owners, loads, stores, sends,
):
    d = lax.axis_index("dom")
    first_lane = (lax.axis_index("tp") == 0).astype(jnp.float32)
    tile = DECODE_STEPS * heads
    queries = per_device * tile
    small = per_device * DECODE_STEPS
    homes = (d, chip_mate(d), next_chip(d))
    width_q, width_k = heads * HEAD_SIZE, groups * HEAD_SIZE
    chunks = 8
    depth = wq.shape[0] // chunks

    def load(j, c):
        return pltpu.make_async_copy(cache.at[c, j], held.at[c, j], loads.at[c, j])

    def clear(j, carry):
        lists[j] = -1
        return carry

    lax.fori_loop(0, per_device, clear, 0)
    for h, home in enumerate(homes):
        there = (home >= 0) & (home < peers)
        start = jnp.clip(home, 0, peers - 1) * per_device

        def enlist(k, carry):
            offset = ancestors[start + k] - d * per_device

            @pl.when(there & (offset >= 0) & (offset < per_device))
            def _():
                slot = h * per_device + k
                lists[per_device + slot] = lists[offset]
                lists[offset] = slot

            return carry

        lax.fori_loop(0, per_device, enlist, 0)

    def flatten(j, count):
        def step(state):
            slot, count = state
            slots[count] = slot
            owners[count] = j
            return lists[per_device + slot], count + 1

        return lax.while_loop(lambda state: state[0] >= 0, step, (lists[j], count))[1]

    count = lax.fori_loop(0, per_device, flatten, jnp.int32(0))
    for extra in range(AT_ONCE - 1):

        @pl.when(count > 0)
        def _():
            slots[count + extra] = slots[count - 1]
            owners[count + extra] = owners[count - 1]

    part[...] = jnp.zeros_like(part)
    results[...] = jnp.zeros_like(results)
    total[...] = jnp.zeros_like(total)
    per_chunk = per_device // chunks

    def project(k, carry):
        for j in range(per_chunk):
            for c in range(2):
                load(k * per_chunk + j, c).start()
        at = pl.ds(pl.multiple_of(k * depth, depth), depth)
        rows = jnp.concatenate([own[:, at], mate[:, at], far[:, at]], 0)
        lanes = 0
        for weight, width in ((wq, width_q), (wk, width_k), (wv, width_k)):
            total[:, lanes : lanes + width] += jnp.dot(
                rows, weight[at, :], preferred_element_type=jnp.float32
            )
            lanes += width
        return carry

    lax.fori_loop(0, chunks, project, 0)

    def turn(x):
        return x * cosine[...] + pltpu.roll(x, HEAD_SIZE // 2, 1) * sine[...]

    block = 2 * groups * small
    for h in range(3):
        mine = slice(h * small, (h + 1) * small)
        for i in range(heads):
            turned[:, i, :] = turn(total[mine, i * HEAD_SIZE : (i + 1) * HEAD_SIZE])
        tokens[h * queries : (h + 1) * queries, :] = (
            turned[...].reshape(queries, HEAD_SIZE).astype(tokens.dtype)
        )
        for g in range(groups):
            lanes = slice(g * HEAD_SIZE, (g + 1) * HEAD_SIZE)
            at = width_q + g * HEAD_SIZE
            key = turn(total[mine, at : at + HEAD_SIZE]).astype(keys.dtype)
            at = at + width_k
            value = total[mine, at : at + HEAD_SIZE].astype(values.dtype)
            at = h * block + g * small
            fresh[at : at + small, :] = key.astype(jnp.float32)
            at = at + groups * small
            fresh[at : at + small, :] = value.astype(jnp.float32)
            if h == 0:
                keys[:, lanes] = key
                values[:, lanes] = value

    row = lax.broadcasted_iota(jnp.int32, (tile, 1), 0)
    lower = (row % heads) < heads // groups
    later = row >= heads
    lane = lax.broadcasted_iota(jnp.int32, (1, HEAD_SIZE), 1)
    scale = 1.0 / math.sqrt(HEAD_SIZE)
    twist = jnp.concatenate([jnp.zeros_like(twist_weight), twist_weight[...]], 0)

    def by_group(at):
        pair = [fresh[pl.ds(at + g * small, 1), :] for g in range(groups)]
        return jnp.where(lower, pair[0], pair[1])

    def scores_of(j, slot):
        query = tokens[pl.ds(pl.multiple_of(slot * tile, tile), tile), :]
        none = jnp.zeros_like(query)
        wide = jnp.concatenate([jnp.where(lower, query, none), jnp.where(lower, none, query)], 1)
        scores = (
            lax.dot_general(
                wide, held[0, j], (((1,), (1,)), ((), ())), preferred_element_type=jnp.float32
            )
            * scale
        )
        return query.astype(jnp.float32), scores

    def weights_of(scores):
        maxima = jnp.max(scores, 1, keepdims=True)
        return maxima, jnp.exp(scores - maxima)

    def finish(j, slot, query, maxima, totals, both):
        weighted = jnp.where(lower, both[:, :HEAD_SIZE], both[:, HEAD_SIZE:])
        at = (slot // per_device) * block + (slot % per_device) * DECODE_STEPS
        new = [
            jnp.sum(query * by_group(at + u), 1, keepdims=True) * scale
            for u in range(DECODE_STEPS)
        ]
        new[1] = jnp.where(later, new[1], -jnp.inf)
        peak = jnp.maximum(maxima, jnp.maximum(new[0], new[1]))
        carried = jnp.exp(maxima - peak)
        numerator = carried * weighted
        denominator = carried * totals
        for u in range(DECODE_STEPS):
            share = jnp.exp(new[u] - peak)
            numerator = numerator + share * by_group(at + groups * small + u)
            denominator = denominator + share
        outputs = numerator / denominator
        results[pl.ds(pl.multiple_of(slot * tile, tile), tile), :] = outputs.astype(jnp.bfloat16)
        twisted = jnp.sum(outputs * twist, 0, keepdims=True)
        less = jnp.where(lane == 0, parent_twist[j] * first_lane, 0.0)
        part[pl.ds(slot, 1), :] = twisted - less

    def store(k, j, c):
        return pltpu.make_async_copy(held.at[c, j], placed.at[c, k], stores.at[c, k])

    def arrive(j, carry):
        for c in range(2):
            load(j, c).wait()

        def step(slot):
            @pl.when(slot < per_device)
            def _():
                for c in range(2):
                    store(slot, j, c).start()

            return lists[per_device + slot]

        lax.while_loop(lambda slot: slot >= 0, step, lists[j])
        return carry

    def serve(step, loaded):
        at = step * AT_ONCE
        last = owners[at + AT_ONCE - 1] + 1
        lax.fori_loop(loaded, last, arrive, 0)
        jobs = [(owners[at + i], slots[at + i]) for i in range(AT_ONCE)]
        scored = [scores_of(*job) for job in jobs]
        weights = [weights_of(scores) for _, scores in scored]
        totals = [jnp.sum(expo, 1, keepdims=True) for _, expo in weights]
        both = [
            jnp.dot(expo.astype(jnp.bfloat16), held[1, job[0]], preferred_element_type=jnp.float32)
            for job, (_, expo) in zip(jobs, weights)
        ]
        for i, job in enumerate(jobs):
            finish(*job, scored[i][0], weights[i][0], totals[i], both[i])
        return last

    loaded = lax.fori_loop(0, (count + AT_ONCE - 1) // AT_ONCE, serve, jnp.int32(0))
    lax.fori_loop(loaded, per_device, arrive, 0)
    skip = PIECES[0]
    copies = [
        pltpu.make_async_copy(held.at[c, picks[skip + i]], sent.at[c, i], sends.at[c, i])
        for i in range(sent.shape[1])
        for c in range(2)
    ]
    for copy in copies:
        copy.start()
    sums = jnp.sum(jnp.transpose(part[...]), 0, keepdims=True)
    spread[...] = jnp.zeros_like(spread)
    for h, home in enumerate(homes):
        share = sums[:, h * per_device : (h + 1) * per_device]
        if h == 0:
            share = share + jnp.sum(log_ratio[...], 0, keepdims=True) * first_lane

        @pl.when((home >= 0) & (home < peers))
        def _():
            spread[pl.ds(jnp.clip(home, 0, peers - 1), 1), :] = share

    out_own[...] = results[:queries, :]
    out_others[...] = results[queries:, :]

    def settle(k, carry):
        offset = ancestors[d * per_device + k] - d * per_device

        @pl.when((offset >= 0) & (offset < per_device))
        def _():
            for c in range(2):
                store(k, offset, c).wait()

        return carry

    lax.fori_loop(0, per_device, settle, 0)
    for copy in copies:
        copy.wait()


def serve(ancestors, picks, parent_twist, log_ratio, twist_weight, own, mate, far, wq, wk, wv, cache, peers):
    per_device, anchor_point = cache.shape[1:3]
    heads, groups = wq.shape[1] // HEAD_SIZE, wk.shape[1] // HEAD_SIZE
    tile = DECODE_STEPS * heads
    queries = per_device * tile
    small = per_device * DECODE_STEPS
    cosine, sine = rope_tables(small, anchor_point)
    columns = wq.shape[1] + wk.shape[1] + wv.shape[1]
    return pl.pallas_call(
        functools.partial(serve_kernel, peers, per_device, heads, groups),
        out_shape=(
            jax.ShapeDtypeStruct((small, groups * HEAD_SIZE), jnp.bfloat16),
            jax.ShapeDtypeStruct((small, groups * HEAD_SIZE), jnp.bfloat16),
            jax.ShapeDtypeStruct((queries, HEAD_SIZE), jnp.bfloat16),
            jax.ShapeDtypeStruct((2 * queries, HEAD_SIZE), jnp.bfloat16),
            jax.ShapeDtypeStruct((peers, per_device), jnp.float32),
            pltpu.HBM(cache.shape, cache.dtype),
            pltpu.HBM((2, PIECES[1], *cache.shape[2:]), cache.dtype),
        ),
        in_specs=[SMEM, SMEM, SMEM] + [VMEM] * 10 + [HBM],
        out_specs=(VMEM, VMEM, VMEM, VMEM, VMEM, HBM, HBM),
        scratch_shapes=[
            pltpu.VMEM(cache.shape, cache.dtype),
            pltpu.VMEM((3 * small, columns), jnp.float32),
            pltpu.VMEM((small, heads, HEAD_SIZE), jnp.float32),
            pltpu.VMEM((3 * queries, HEAD_SIZE), jnp.bfloat16),
            pltpu.VMEM((3 * 2 * groups * small, HEAD_SIZE), jnp.float32),
            pltpu.VMEM((3 * queries, HEAD_SIZE), jnp.bfloat16),
            pltpu.VMEM((HEAD_SIZE, HEAD_SIZE), jnp.float32),
            pltpu.SMEM((4 * per_device,), jnp.int32),
            pltpu.SMEM((3 * per_device + AT_ONCE,), jnp.int32),
            pltpu.SMEM((3 * per_device + AT_ONCE,), jnp.int32),
            pltpu.SemaphoreType.DMA((2, per_device)),
            pltpu.SemaphoreType.DMA((2, per_device)),
            pltpu.SemaphoreType.DMA((2, PIECES[1])),
        ],
        compiler_params=pltpu.CompilerParams(vmem_limit_bytes=28 * 2**20),
        cost_estimate=LIGHT,
        name="serve",
    )(
        ancestors, picks, parent_twist, log_ratio, twist_weight, own, mate, far, cosine, sine,
        wq, wk, wv, cache,
    )


def normalise_kernel(terms, *refs):
    *parts, out = refs
    del terms
    total = parts[0][...]
    for part in parts[1:]:
        total = total + part[...]
    peak = jnp.max(total, keepdims=True)
    mass = jnp.sum(jnp.exp(total - peak), keepdims=True)
    row = lax.broadcasted_iota(jnp.int32, total.shape, 0)
    mine = jnp.sum(jnp.where(row == lax.axis_index("dom"), total, 0.0), 0, keepdims=True)
    out[...] = mine - (peak + jnp.log(mass))


def normalise(parts):
    return pl.pallas_call(
        functools.partial(normalise_kernel, len(parts)),
        out_shape=jax.ShapeDtypeStruct((1, parts[0].shape[1]), jnp.float32),
        in_specs=[VMEM] * len(parts),
        out_specs=VMEM,
        compiler_params=SMALL,
        cost_estimate=LIGHT,
        name="normalise",
    )(*parts)


def total_but_y(x, peers):
    side = math.isqrt(peers // 2)
    on_chip = [(i, i ^ 1) for i in range(peers)]
    x = x + lax.ppermute(x, "dom", on_chip)
    ring, hop = lax.axis_size("tp"), 1
    while hop < ring:
        x = x + lax.ppermute(x, "tp", [(i, i ^ hop) for i in range(ring)])
        hop *= 2
    step = 2 * side
    pairs = [(i, (i + step * (1 - 2 * (i % 2))) % peers) for i in range(peers)]
    first = lax.ppermute(x, "dom", pairs)
    return x + first + lax.ppermute(first, "dom", pairs) + lax.ppermute(first, "dom", on_chip)


def parts_along_y(x, peers):
    step = 2 * math.isqrt(peers // 2)
    parts = [x]
    for hop in range(2, step, 2):
        pairs = [(i, i // step * step + (i + hop) % step) for i in range(peers)]
        parts.append(lax.ppermute(x, "dom", pairs))
    return parts


def shards(
    cache,
    hidden,
    query_weight,
    key_projection_weight,
    value_projection_weight,
    twist_weight,
    parent_twist,
    log_ratio,
    ancestors,
):
    per_device = hidden.shape[0]
    heads = query_weight.shape[1] // HEAD_SIZE
    groups = key_projection_weight.shape[1] // HEAD_SIZE
    peers = lax.axis_size("dom")
    d = lax.axis_index("dom")
    on_chip = [(i, i ^ 1) for i in range(peers)]
    off_chip = [(i, i - 1 + 2 * (i % 2)) for i in range(1, peers - 1)]
    beside = [(i, i + 2 - 4 * (i % 2)) for i in range(peers) if 0 <= i + 2 - 4 * (i % 2) < peers]
    rows = hidden.reshape(per_device * DECODE_STEPS, -1)
    far_rows = lax.ppermute(rows, "dom", off_chip)
    mate_rows = lax.ppermute(rows, "dom", on_chip)
    count, picks, ranks = plan(ancestors, peers, per_device)
    sent, far_rows = lax.optimization_barrier((gather(picks, cache, 0, PIECES[0]), far_rows))
    first = lax.ppermute(sent, "dom", off_chip)
    late_cache, far_rows, mate_rows = lax.optimization_barrier((cache, far_rows, mate_rows))
    mate_cache = lax.ppermute(late_cache, "dom", on_chip)
    keys, values, own_part, others_part, spread, out, sent = serve(
        ancestors, picks, parent_twist, log_ratio.T, twist_weight.reshape(heads, HEAD_SIZE),
        rows, mate_rows, far_rows, query_weight, key_projection_weight, value_projection_weight,
        cache, peers,
    )
    second = lax.ppermute(sent, "dom", off_chip)
    spread = total_but_y(spread, peers)
    mate_part, far_part = jnp.split(lax.ppermute(others_part, "dom", on_chip), 2)
    far_part = lax.ppermute(far_part, "dom", beside)
    owner = lax.dynamic_slice_in_dim(ancestors, d * per_device, per_device) // per_device
    owner = jnp.repeat(owner, DECODE_STEPS * heads)[:, None]
    attention = jnp.where(
        owner == d, own_part, jnp.where(owner == chip_mate(d), mate_part, far_part)
    ).reshape(per_device, DECODE_STEPS, heads * HEAD_SIZE)
    out = place_first(ancestors, ranks, mate_cache, first, out)
    spread, out = lax.optimization_barrier((spread, out))
    log_weights = normalise(parts_along_y(spread, peers)).reshape(per_device)
    fresh = jnp.stack([keys, values]).reshape(2, per_device, DECODE_STEPS, groups * HEAD_SIZE)

    def more(size):
        def branch(cache, picks, ranks, out):
            came = lax.ppermute(gather(picks, cache, ALWAYS, size), "dom", off_chip)
            return place_more(ranks, came, out, ALWAYS)

        return branch

    out = lax.switch(
        jnp.maximum(count[0] - ALWAYS, 0),
        [lambda cache, picks, ranks, out: out] + [more(i + 1) for i in range(per_device - ALWAYS)],
        cache, picks, ranks, out,
    )
    out = place_more(ranks, second, out, PIECES[0])
    return (out, fresh, attention, log_weights)


def solution(mesh):
    return jax.shard_map(
        shards,
        mesh=mesh,
        in_specs=(
            P(None, "dom", None, "tp"),
            P("dom", None, None),
            P(None, "tp"),
            P(None, "tp"),
            P(None, "tp"),
            P("tp"),
            P("dom"),
            P("dom", None),
            P(),
        ),
        out_specs=(
            P(None, "dom", None, "tp"),
            P(None, "dom", None, "tp"),
            P("dom", None, "tp"),
            P("dom"),
        ),
        check_vma=False,
    )
```

```python
import functools
import math

import jax
import jax.numpy as jnp
import numpy as np
from jax import lax
from jax.experimental import pallas as pl
from jax.experimental.pallas import tpu as pltpu
from jax.sharding import PartitionSpec as P

HEAD_SIZE = 128
DECODE_STEPS = 2
ROPE_BASE = 500000.0
PIECES = (6, 2)
ALWAYS = sum(PIECES)
AT_ONCE = 6

SMEM = pl.BlockSpec(memory_space=pltpu.SMEM)
VMEM = pl.BlockSpec(memory_space=pltpu.VMEM)
ANY = pl.BlockSpec(memory_space=pl.ANY)
HBM = pl.BlockSpec(memory_space=pltpu.HBM)
SMALL = pltpu.CompilerParams(vmem_limit_bytes=2 * 2**20)
LIGHT = pl.CostEstimate(flops=0, bytes_accessed=0, transcendentals=0)


def chip_mate(d):
    return d + 1 - 2 * (d % 2)


def next_chip(d):
    return d - 1 + 2 * (d % 2)


def rope_tables(rows, anchor_point):
    half = HEAD_SIZE // 2
    frequency = np.exp(
        np.arange(half, dtype=np.float32) * np.float32(-2.0 * math.log(ROPE_BASE) / HEAD_SIZE)
    ).astype(np.float32)
    positions = (anchor_point + np.arange(rows) % DECODE_STEPS).astype(np.float32)
    angles = (positions[:, None] * frequency[None, :]).astype(np.float32)
    cosine = np.cos(angles).astype(np.float32)
    sine = np.sin(angles).astype(np.float32)
    return np.concatenate([cosine, cosine], 1), np.concatenate([-sine, sine], 1)


def bit_count(mask):
    mask = mask - ((mask >> 1) & 0x55555555)
    mask = (mask & 0x33333333) + ((mask >> 2) & 0x33333333)
    mask = (mask + (mask >> 4)) & 0x0F0F0F0F
    return (mask * 0x01010101) >> 24


def plan_kernel(peers, per_device, ancestors, grid, count, picks, ranks):
    d = lax.axis_index("dom")
    shape = grid.shape
    flat = lax.broadcasted_iota(jnp.int32, shape, 0) * shape[1] + lax.broadcasted_iota(
        jnp.int32, shape, 1
    )
    home = flat // per_device
    offset = grid[...] - next_chip(home) * per_device
    inside = (offset >= 0) & (offset < per_device)
    bits = jnp.where(inside, jnp.int32(1) << (offset & (per_device - 1)), 0)
    shift = 1
    while shift < per_device:
        bits = bits | pltpu.roll(bits, shape[1] - shift, 1)
        shift *= 2
    most = jnp.where(flat % per_device == 0, bit_count(bits), 0)
    count[0] = jnp.max(most.astype(jnp.float32)).astype(jnp.int32)

    def needed(home, owner):
        mask = jnp.int32(0)
        for k in range(per_device):
            offset = ancestors[home * per_device + k] - owner * per_device
            inside = (offset >= 0) & (offset < per_device)
            mask = mask | jnp.where(inside, jnp.int32(1) << (offset & (per_device - 1)), 0)
        return mask

    there = next_chip(d)
    mask = needed(jnp.clip(there, 0, peers - 1), d)
    position = jnp.int32(0)
    for j in range(per_device):
        picks[j] = 0
    for j in range(per_device):
        picks[position] = j
        position = position + ((mask >> j) & 1)
    mask = needed(d, there)
    for k in range(per_device):
        offset = ancestors[d * per_device + k] - there * per_device
        inside = (offset >= 0) & (offset < per_device)
        below = (jnp.int32(1) << (offset & (per_device - 1))) - 1
        ranks[k] = jnp.where(inside, bit_count(mask & below), -1)


def plan(ancestors, peers, per_device):
    return pl.pallas_call(
        functools.partial(plan_kernel, peers, per_device),
        out_shape=(
            jax.ShapeDtypeStruct((1,), jnp.int32),
            jax.ShapeDtypeStruct((per_device,), jnp.int32),
            jax.ShapeDtypeStruct((per_device,), jnp.int32),
        ),
        in_specs=[SMEM, VMEM],
        out_specs=(SMEM, SMEM, SMEM),
        cost_estimate=LIGHT,
        name="plan",
    )(ancestors, ancestors.reshape(-1, 128))


def gather_kernel(skip, size, picks, cache, sent, sems):
    def load(i, c):
        return pltpu.make_async_copy(cache.at[c, picks[skip + i]], sent.at[c, i], sems.at[c, i])

    def each(act):
        def body(i, carry):
            for c in range(2):
                act(load(i, c))
            return carry

        lax.fori_loop(0, size, body, 0)

    each(lambda copy: copy.start())
    each(lambda copy: copy.wait())


def gather(picks, cache, skip, size):
    shape = (2, size, *cache.shape[2:])
    return pl.pallas_call(
        functools.partial(gather_kernel, skip, size),
        out_shape=pltpu.VMEM(shape, cache.dtype),
        in_specs=[SMEM, HBM],
        out_specs=VMEM,
        scratch_shapes=[pltpu.SemaphoreType.DMA((2, size))],
        compiler_params=pltpu.CompilerParams(vmem_limit_bytes=12 * 2**20),
        cost_estimate=pl.CostEstimate(
            flops=0, bytes_accessed=16 * 2**20, transcendentals=0
        ),
        name="gather",
    )(picks, cache)


def place_kernel(per_device, find, tables, *refs):
    numbers, refs = refs[:tables], refs[tables:]
    *sources, _, out, held, loads, stores = refs
    d = lax.axis_index("dom")

    def each(act):
        def body(k, carry):
            for source, (there, at) in zip(sources, find(numbers, d, k)):

                @pl.when(there)
                def _():
                    for c in range(2):
                        act(source, at, k, c)

            return carry

        lax.fori_loop(0, per_device, body, 0)

    def load(source, at, k, c):
        return pltpu.make_async_copy(source.at[c, at], held.at[c, k], loads.at[c, k])

    def store(k, c):
        return pltpu.make_async_copy(held.at[c, k], out.at[c, k], stores.at[c, k])

    def forward(source, at, k, c):
        load(source, at, k, c).wait()
        store(k, c).start()

    each(lambda source, at, k, c: load(source, at, k, c).start())
    each(forward)
    each(lambda source, at, k, c: store(k, c).wait())


def place(find, numbers, sources, placed, name):
    per_device = placed.shape[1]
    operands = [*numbers, *sources, placed]
    return pl.pallas_call(
        functools.partial(place_kernel, per_device, find, len(numbers)),
        out_shape=pltpu.HBM(placed.shape, placed.dtype),
        in_specs=[SMEM] * len(numbers) + [ANY] * len(sources) + [HBM],
        out_specs=HBM,
        scratch_shapes=[
            pltpu.VMEM(placed.shape, placed.dtype),
            pltpu.SemaphoreType.DMA((2, per_device)),
            pltpu.SemaphoreType.DMA((2, per_device)),
        ],
        input_output_aliases={len(operands) - 1: 0},
        compiler_params=pltpu.CompilerParams(vmem_limit_bytes=12 * 2**20),
        cost_estimate=LIGHT,
        name=name,
    )(*operands)


def place_first(ancestors, ranks, mate, came, placed):
    per_device, size = placed.shape[1], came.shape[1]

    def find(numbers, d, k):
        ancestors, ranks = numbers
        offset = ancestors[d * per_device + k] - chip_mate(d) * per_device
        yield (offset >= 0) & (offset < per_device), offset
        yield (ranks[k] >= 0) & (ranks[k] < size), ranks[k]

    return place(find, [ancestors, ranks], [mate, came], placed, "place_first")


def place_more(ranks, came, placed, skip):
    size = came.shape[1]

    def find(numbers, d, k):
        rank = numbers[0][k] - skip
        yield (rank >= 0) & (rank < size), rank

    return place(find, [ranks], [came], placed, "place_more")


def serve_kernel(
    peers, per_device, heads, groups,
    ancestors, picks, parent_twist, log_ratio, twist_weight, own, mate, far, cosine, sine,
    wq, wk, wv, cache,
    keys, values, out_own, out_others, spread, placed, sent,
    held, total, turned, tokens, fresh, results,
    part, lists, slots, owners, loads, stores, sends,
):
    d = lax.axis_index("dom")
    first_lane = (lax.axis_index("tp") == 0).astype(jnp.float32)
    tile = DECODE_STEPS * heads
    queries = per_device * tile
    small = per_device * DECODE_STEPS
    homes = (d, chip_mate(d), next_chip(d))
    width_q, width_k = heads * HEAD_SIZE, groups * HEAD_SIZE
    chunks = 8
    depth = wq.shape[0] // chunks

    def load(j, c):
        return pltpu.make_async_copy(cache.at[c, j], held.at[c, j], loads.at[c, j])

    def clear(j, carry):
        lists[j] = -1
        return carry

    lax.fori_loop(0, per_device, clear, 0)
    for h, home in enumerate(homes):
        there = (home >= 0) & (home < peers)
        start = jnp.clip(home, 0, peers - 1) * per_device

        def enlist(k, carry):
            offset = ancestors[start + k] - d * per_device

            @pl.when(there & (offset >= 0) & (offset < per_device))
            def _():
                slot = h * per_device + k
                lists[per_device + slot] = lists[offset]
                lists[offset] = slot

            return carry

        lax.fori_loop(0, per_device, enlist, 0)

    def flatten(j, count):
        def step(state):
            slot, count = state
            slots[count] = slot
            owners[count] = j
            return lists[per_device + slot], count + 1

        return lax.while_loop(lambda state: state[0] >= 0, step, (lists[j], count))[1]

    count = lax.fori_loop(0, per_device, flatten, jnp.int32(0))
    for extra in range(AT_ONCE - 1):

        @pl.when(count > 0)
        def _():
            slots[count + extra] = slots[count - 1]
            owners[count + extra] = owners[count - 1]

    part[...] = jnp.zeros_like(part)
    results[...] = jnp.zeros_like(results)
    total[...] = jnp.zeros_like(total)
    per_chunk = per_device // chunks

    def project(k, carry):
        for j in range(per_chunk):
            for c in range(2):
                load(k * per_chunk + j, c).start()
        at = pl.ds(pl.multiple_of(k * depth, depth), depth)
        rows = jnp.concatenate([own[:, at], mate[:, at], far[:, at]], 0)
        lanes = 0
        for weight, width in ((wq, width_q), (wk, width_k), (wv, width_k)):
            total[:, lanes : lanes + width] += jnp.dot(
                rows, weight[at, :], preferred_element_type=jnp.float32
            )
            lanes += width
        return carry

    lax.fori_loop(0, chunks, project, 0)

    def turn(x):
        return x * cosine[...] + pltpu.roll(x, HEAD_SIZE // 2, 1) * sine[...]

    block = 2 * groups * small
    for h in range(3):
        mine = slice(h * small, (h + 1) * small)
        for i in range(heads):
            turned[:, i, :] = turn(total[mine, i * HEAD_SIZE : (i + 1) * HEAD_SIZE])
        tokens[h * queries : (h + 1) * queries, :] = (
            turned[...].reshape(queries, HEAD_SIZE).astype(tokens.dtype)
        )
        for g in range(groups):
            lanes = slice(g * HEAD_SIZE, (g + 1) * HEAD_SIZE)
            at = width_q + g * HEAD_SIZE
            key = turn(total[mine, at : at + HEAD_SIZE]).astype(keys.dtype)
            at = at + width_k
            value = total[mine, at : at + HEAD_SIZE].astype(values.dtype)
            at = h * block + g * small
            fresh[at : at + small, :] = key.astype(jnp.float32)
            at = at + groups * small
            fresh[at : at + small, :] = value.astype(jnp.float32)
            if h == 0:
                keys[:, lanes] = key
                values[:, lanes] = value

    row = lax.broadcasted_iota(jnp.int32, (tile, 1), 0)
    lower = (row % heads) < heads // groups
    later = row >= heads
    lane = lax.broadcasted_iota(jnp.int32, (1, HEAD_SIZE), 1)
    scale = 1.0 / math.sqrt(HEAD_SIZE)
    twist = jnp.concatenate([jnp.zeros_like(twist_weight), twist_weight[...]], 0)

    def by_group(at):
        pair = [fresh[pl.ds(at + g * small, 1), :] for g in range(groups)]
        return jnp.where(lower, pair[0], pair[1])

    def scores_of(j, slot):
        query = tokens[pl.ds(pl.multiple_of(slot * tile, tile), tile), :]
        none = jnp.zeros_like(query)
        wide = jnp.concatenate([jnp.where(lower, query, none), jnp.where(lower, none, query)], 1)
        scores = (
            lax.dot_general(
                wide, held[0, j], (((1,), (1,)), ((), ())), preferred_element_type=jnp.float32
            )
            * scale
        )
        return query.astype(jnp.float32), scores

    def weights_of(scores):
        maxima = jnp.max(scores, 1, keepdims=True)
        return maxima, jnp.exp(scores - maxima)

    def finish(j, slot, query, maxima, totals, both):
        weighted = jnp.where(lower, both[:, :HEAD_SIZE], both[:, HEAD_SIZE:])
        at = (slot // per_device) * block + (slot % per_device) * DECODE_STEPS
        new = [
            jnp.sum(query * by_group(at + u), 1, keepdims=True) * scale
            for u in range(DECODE_STEPS)
        ]
        new[1] = jnp.where(later, new[1], -jnp.inf)
        peak = jnp.maximum(maxima, jnp.maximum(new[0], new[1]))
        carried = jnp.exp(maxima - peak)
        numerator = carried * weighted
        denominator = carried * totals
        for u in range(DECODE_STEPS):
            share = jnp.exp(new[u] - peak)
            numerator = numerator + share * by_group(at + groups * small + u)
            denominator = denominator + share
        outputs = numerator / denominator
        results[pl.ds(pl.multiple_of(slot * tile, tile), tile), :] = outputs.astype(jnp.bfloat16)
        twisted = jnp.sum(outputs * twist, 0, keepdims=True)
        less = jnp.where(lane == 0, parent_twist[j] * first_lane, 0.0)
        part[pl.ds(slot, 1), :] = twisted - less

    def store(k, j, c):
        return pltpu.make_async_copy(held.at[c, j], placed.at[c, k], stores.at[c, k])

    def arrive(j, carry):
        for c in range(2):
            load(j, c).wait()

        def step(slot):
            @pl.when(slot < per_device)
            def _():
                for c in range(2):
                    store(slot, j, c).start()

            return lists[per_device + slot]

        lax.while_loop(lambda slot: slot >= 0, step, lists[j])
        return carry

    def serve(step, loaded):
        at = step * AT_ONCE
        last = owners[at + AT_ONCE - 1] + 1
        lax.fori_loop(loaded, last, arrive, 0)
        jobs = [(owners[at + i], slots[at + i]) for i in range(AT_ONCE)]
        scored = [scores_of(*job) for job in jobs]
        weights = [weights_of(scores) for _, scores in scored]
        totals = [jnp.sum(expo, 1, keepdims=True) for _, expo in weights]
        both = [
            jnp.dot(expo.astype(jnp.bfloat16), held[1, job[0]], preferred_element_type=jnp.float32)
            for job, (_, expo) in zip(jobs, weights)
        ]
        for i, job in enumerate(jobs):
            finish(*job, scored[i][0], weights[i][0], totals[i], both[i])
        return last

    loaded = lax.fori_loop(0, (count + AT_ONCE - 1) // AT_ONCE, serve, jnp.int32(0))
    lax.fori_loop(loaded, per_device, arrive, 0)
    skip = PIECES[0]
    copies = [
        pltpu.make_async_copy(held.at[c, picks[skip + i]], sent.at[c, i], sends.at[c, i])
        for i in range(sent.shape[1])
        for c in range(2)
    ]
    for copy in copies:
        copy.start()
    sums = jnp.sum(jnp.transpose(part[...]), 0, keepdims=True)
    spread[...] = jnp.zeros_like(spread)
    for h, home in enumerate(homes):
        share = sums[:, h * per_device : (h + 1) * per_device]
        if h == 0:
            share = share + jnp.sum(log_ratio[...], 0, keepdims=True) * first_lane

        @pl.when((home >= 0) & (home < peers))
        def _():
            spread[pl.ds(jnp.clip(home, 0, peers - 1), 1), :] = share

    out_own[...] = results[:queries, :]
    out_others[...] = results[queries:, :]

    def settle(k, carry):
        offset = ancestors[d * per_device + k] - d * per_device

        @pl.when((offset >= 0) & (offset < per_device))
        def _():
            for c in range(2):
                store(k, offset, c).wait()

        return carry

    lax.fori_loop(0, per_device, settle, 0)
    for copy in copies:
        copy.wait()


def serve(ancestors, picks, parent_twist, log_ratio, twist_weight, own, mate, far, wq, wk, wv, cache, peers):
    per_device, anchor_point = cache.shape[1:3]
    heads, groups = wq.shape[1] // HEAD_SIZE, wk.shape[1] // HEAD_SIZE
    tile = DECODE_STEPS * heads
    queries = per_device * tile
    small = per_device * DECODE_STEPS
    cosine, sine = rope_tables(small, anchor_point)
    columns = wq.shape[1] + wk.shape[1] + wv.shape[1]
    return pl.pallas_call(
        functools.partial(serve_kernel, peers, per_device, heads, groups),
        out_shape=(
            jax.ShapeDtypeStruct((small, groups * HEAD_SIZE), jnp.bfloat16),
            jax.ShapeDtypeStruct((small, groups * HEAD_SIZE), jnp.bfloat16),
            jax.ShapeDtypeStruct((queries, HEAD_SIZE), jnp.bfloat16),
            jax.ShapeDtypeStruct((2 * queries, HEAD_SIZE), jnp.bfloat16),
            jax.ShapeDtypeStruct((peers, per_device), jnp.float32),
            pltpu.HBM(cache.shape, cache.dtype),
            pltpu.HBM((2, PIECES[1], *cache.shape[2:]), cache.dtype),
        ),
        in_specs=[SMEM, SMEM, SMEM] + [VMEM] * 10 + [HBM],
        out_specs=(VMEM, VMEM, VMEM, VMEM, VMEM, HBM, HBM),
        scratch_shapes=[
            pltpu.VMEM(cache.shape, cache.dtype),
            pltpu.VMEM((3 * small, columns), jnp.float32),
            pltpu.VMEM((small, heads, HEAD_SIZE), jnp.float32),
            pltpu.VMEM((3 * queries, HEAD_SIZE), jnp.bfloat16),
            pltpu.VMEM((3 * 2 * groups * small, HEAD_SIZE), jnp.float32),
            pltpu.VMEM((3 * queries, HEAD_SIZE), jnp.bfloat16),
            pltpu.VMEM((HEAD_SIZE, HEAD_SIZE), jnp.float32),
            pltpu.SMEM((4 * per_device,), jnp.int32),
            pltpu.SMEM((3 * per_device + AT_ONCE,), jnp.int32),
            pltpu.SMEM((3 * per_device + AT_ONCE,), jnp.int32),
            pltpu.SemaphoreType.DMA((2, per_device)),
            pltpu.SemaphoreType.DMA((2, per_device)),
            pltpu.SemaphoreType.DMA((2, PIECES[1])),
        ],
        compiler_params=pltpu.CompilerParams(vmem_limit_bytes=28 * 2**20),
        cost_estimate=LIGHT,
        name="serve",
    )(
        ancestors, picks, parent_twist, log_ratio, twist_weight, own, mate, far, cosine, sine,
        wq, wk, wv, cache,
    )


def normalise_kernel(terms, *refs):
    *parts, out = refs
    del terms
    total = parts[0][...]
    for part in parts[1:]:
        total = total + part[...]
    peak = jnp.max(total, keepdims=True)
    mass = jnp.sum(jnp.exp(total - peak), keepdims=True)
    row = lax.broadcasted_iota(jnp.int32, total.shape, 0)
    mine = jnp.sum(jnp.where(row == lax.axis_index("dom"), total, 0.0), 0, keepdims=True)
    out[...] = mine - (peak + jnp.log(mass))


def normalise(parts):
    return pl.pallas_call(
        functools.partial(normalise_kernel, len(parts)),
        out_shape=jax.ShapeDtypeStruct((1, parts[0].shape[1]), jnp.float32),
        in_specs=[VMEM] * len(parts),
        out_specs=VMEM,
        compiler_params=SMALL,
        cost_estimate=LIGHT,
        name="normalise",
    )(*parts)


def total_but_y(x, peers):
    side = math.isqrt(peers // 2)
    on_chip = [(i, i ^ 1) for i in range(peers)]
    x = x + lax.ppermute(x, "dom", on_chip)
    ring, hop = lax.axis_size("tp"), 1
    while hop < ring:
        x = x + lax.ppermute(x, "tp", [(i, i ^ hop) for i in range(ring)])
        hop *= 2
    step = 2 * side
    pairs = [(i, (i + step * (1 - 2 * (i % 2))) % peers) for i in range(peers)]
    first = lax.ppermute(x, "dom", pairs)
    return x + first + lax.ppermute(first, "dom", pairs) + lax.ppermute(first, "dom", on_chip)


def parts_along_y(x, peers):
    step = 2 * math.isqrt(peers // 2)
    parts = [x]
    for hop in range(2, step, 2):
        pairs = [(i, i // step * step + (i + hop) % step) for i in range(peers)]
        parts.append(lax.ppermute(x, "dom", pairs))
    return parts


def shards(
    cache,
    hidden,
    query_weight,
    key_projection_weight,
    value_projection_weight,
    twist_weight,
    parent_twist,
    log_ratio,
    ancestors,
):
    per_device = hidden.shape[0]
    heads = query_weight.shape[1] // HEAD_SIZE
    groups = key_projection_weight.shape[1] // HEAD_SIZE
    peers = lax.axis_size("dom")
    d = lax.axis_index("dom")
    on_chip = [(i, i ^ 1) for i in range(peers)]
    off_chip = [(i, i - 1 + 2 * (i % 2)) for i in range(1, peers - 1)]
    beside = [(i, i + 2 - 4 * (i % 2)) for i in range(peers) if 0 <= i + 2 - 4 * (i % 2) < peers]
    rows = hidden.reshape(per_device * DECODE_STEPS, -1)
    far_rows = lax.ppermute(rows, "dom", off_chip)
    mate_rows = lax.ppermute(rows, "dom", on_chip)
    count, picks, ranks = plan(ancestors, peers, per_device)
    sent, far_rows = lax.optimization_barrier((gather(picks, cache, 0, PIECES[0]), far_rows))
    first = lax.ppermute(sent, "dom", off_chip)
    late_cache, far_rows, mate_rows = lax.optimization_barrier((cache, far_rows, mate_rows))
    mate_cache = lax.ppermute(late_cache, "dom", on_chip)
    keys, values, own_part, others_part, spread, out, sent = serve(
        ancestors, picks, parent_twist, log_ratio.T, twist_weight.reshape(heads, HEAD_SIZE),
        rows, mate_rows, far_rows, query_weight, key_projection_weight, value_projection_weight,
        cache, peers,
    )
    second = lax.ppermute(sent, "dom", off_chip)
    spread = total_but_y(spread, peers)
    mate_part, far_part = jnp.split(lax.ppermute(others_part, "dom", on_chip), 2)
    far_part = lax.ppermute(far_part, "dom", beside)
    owner = lax.dynamic_slice_in_dim(ancestors, d * per_device, per_device) // per_device
    owner = jnp.repeat(owner, DECODE_STEPS * heads)[:, None]
    attention = jnp.where(
        owner == d, own_part, jnp.where(owner == chip_mate(d), mate_part, far_part)
    ).reshape(per_device, DECODE_STEPS, heads * HEAD_SIZE)
    out = place_first(ancestors, ranks, mate_cache, first, out)
    spread, out = lax.optimization_barrier((spread, out))
    log_weights = normalise(parts_along_y(spread, peers)).reshape(per_device)
    fresh = jnp.stack([keys, values]).reshape(2, per_device, DECODE_STEPS, groups * HEAD_SIZE)

    def more(size):
        def branch(cache, picks, ranks, out):
            came = lax.ppermute(gather(picks, cache, ALWAYS, size), "dom", off_chip)
            return place_more(ranks, came, out, ALWAYS)

        return branch

    out = lax.switch(
        jnp.maximum(count[0] - ALWAYS, 0),
        [lambda cache, picks, ranks, out: out] + [more(i + 1) for i in range(per_device - ALWAYS)],
        cache, picks, ranks, out,
    )
    out = place_more(ranks, second, out, PIECES[0])
    return (out, fresh, attention, log_weights)


def solution(mesh):
    return jax.shard_map(
        shards,
        mesh=mesh,
        in_specs=(
            P(None, "dom", None, "tp"),
            P("dom", None, None),
            P(None, "tp"),
            P(None, "tp"),
            P(None, "tp"),
            P("tp"),
            P("dom"),
            P("dom", None),
            P(),
        ),
        out_specs=(
            P(None, "dom", None, "tp"),
            P(None, "dom", None, "tp"),
            P("dom", None, "tp"),
            P("dom"),
        ),
        check_vma=False,
    )
```
